32 devices in a mesh: wide: 16 (over z, y, x), narrow: 2 (over core).
Axes of the slice: x: 2, y: 2, z: 4, core: 2. Of those that a mesh axis runs over, the one named last changes fastest.
Arguments:
- factor: bfloat16 [4, 2048, 4, 2048], P(None, 'wide', None, 'narrow'), may hold values from -0.0625 to 0.0625
- diag_inverse: float32 [4, 2048, 2048], P(None, 'wide', 'narrow'), as said below
- parent: int32 [15], replicated, may hold values from -1 to 14, as said below
- tile_node: int32 [4, 8], replicated, may hold values from 0 to 14, as said below
- structure: int32 [15, 4, 8], replicated, may hold values from 0 to 1, as said below
Outputs:
- selected_inverse: float32 [4, 2048, 4, 2048], P(None, 'wide', None, 'narrow')
The draws below stay inside these ranges and needn't reach their ends.
Inputs may be any that keep to these rules, and one draw needn't show every extreme that they name: The tree is a complete binary tree of 4 levels; the root's entry is -1, every other supernode's entry is its parent. `tile_node`: level k holds the 2 ** k supernodes at depth k of the tree, each owning 8 / 2 ** k of the level's tile positions. `structure`: an entry is 1 only where the tile's supernode is a strict ancestor of supernode i (dimension 0). `diag_inverse`: Symmetric; each supernode's diagonal block is positive definite.
All inputs are finite; a program needn't handle non-finite values.
Results may differ from the reference program's by a relative error of at most 0.0016.
Values may be sent and summed in bfloat16 or wider, within the bound.
No kernel may reach another device: no remote copies, remote signals or barrier semaphores. Data moves between devices by JAX's collectives and lax.ppermute only.
A program may use at most 192 MiB of HBM per device.

```python
import math
import jax
import jax.numpy as jnp
from jax import lax

LEV = 4
TILE = 256
LT = 8
M = 15
NL = 2048


def tree_layout(key):
    labels = jax.random.permutation(jax.random.fold_in(key, 101), M).astype(jnp.int32)
    heaps = []
    for level_no in range(LEV):
        order = jax.random.permutation(jax.random.fold_in(key, 200 + level_no), LT).astype(jnp.int32)
        heaps.append(2 ** level_no - 1 + order // (LT // 2 ** level_no))
    heap_tile = jnp.stack(heaps).astype(jnp.int32)
    return (labels, heap_tile)


def draw_parent(key, part):
    labels, heap_tile = tree_layout(key)
    position = jnp.arange(M, dtype=jnp.int32)
    upper = jnp.where(position == 0, -1, labels[jnp.maximum(position - 1, 0) // 2])
    return jnp.zeros((M,), jnp.int32).at[labels].set(upper.astype(jnp.int32))


def draw_tile_node(key, part):
    labels, heap_tile = tree_layout(key)
    return labels[heap_tile].astype(jnp.int32)


def draw_structure(key, part):
    labels, heap_tile = tree_layout(key)
    key = jax.random.fold_in(key, 3)
    heap_node = jnp.arange(M, dtype=jnp.int32)
    relation = jnp.zeros((M, LEV, LT), jnp.int32)
    for shift_no in range(1, LEV):
        hit = heap_node[:, None, None] + 1 >> shift_no == heap_tile[None, :, :] + 1
        relation = relation + hit.astype(jnp.int32)
    present = (jax.random.randint(key, (M, LEV, LT), 0, 4) > 0).astype(jnp.int32)
    by_heap = jnp.minimum(relation, 1) * present
    return jnp.zeros((M, LEV, LT), jnp.int32).at[labels].set(by_heap)


def draw_diag_inverse(key, part):
    key = jax.random.fold_in(key, 4)
    first, second = jax.random.split(key, 2)
    base = jax.random.normal(first, (LEV, NL, NL), jnp.float32)
    symmetric = (base + jnp.swapaxes(base, 1, 2)) * (0.2 / math.sqrt(NL))
    diag_vals = jnp.exp(jax.random.uniform(second, (LEV, NL), jnp.float32, 0.0, math.log(3.0)))
    eye_mat = (jnp.arange(NL)[:, None] == jnp.arange(NL)[None, :]).astype(jnp.float32)
    result = symmetric + eye_mat[None, :, :] * diag_vals[:, :, None]
    return result


def shard_levels(key, shape, pieces, low, largest):
    def one(dim, parts):
        draws = jax.random.uniform(jax.random.fold_in(jax.random.fold_in(key, 6), dim), (parts,), jnp.float32, low / len(pieces), largest / len(pieces))
        return jnp.repeat(jnp.exp(draws), shape[dim] // parts).reshape((-1,) + (1,) * (len(shape) - dim - 1))

    gain = one(*pieces[0])
    for cut in pieces[1:]:
        gain = gain * one(*cut)
    return gain


def centred(stream_key, extent, scale, most, pieces=(), kind=jnp.bfloat16):
    gain = shard_levels(stream_key, extent, pieces, -0.22, 0.18) if pieces else 1.0
    array = jax.random.normal(stream_key, extent, jnp.float32) * scale * gain
    return jnp.minimum(jnp.maximum(array, -most), most).astype(kind)


def setup_inputs(seed: int = 0) -> dict:
    streams_of = jax.random.split(jax.random.key(seed), 6)
    return {
        "factor": centred(streams_of[0], (LEV, NL, LEV, NL), (LEV * LT * TILE) ** -0.5, 0.0625, ((1, 16), (3, 2))),
        "diag_inverse": draw_diag_inverse(jax.random.fold_in(streams_of[5], 71), 0),
        "parent": draw_parent(jax.random.fold_in(streams_of[5], 71), 0),
        "tile_node": draw_tile_node(jax.random.fold_in(streams_of[5], 71), 0),
        "structure": draw_structure(jax.random.fold_in(streams_of[5], 71), 0),
    }


def ancestors(parent):
    node_ids = jnp.arange(M, dtype=jnp.int32)
    step_mat = (parent[:, None] == node_ids[None, :]).astype(jnp.float32)
    power_mat = step_mat
    reach = step_mat
    for hop_count in range(LEV - 2):
        power_mat = jnp.dot(power_mat, step_mat, precision=lax.Precision.HIGHEST)
        reach = reach + power_mat
    return reach


def spread_both(mask_tile):
    return jnp.repeat(jnp.repeat(mask_tile, TILE, axis=-2), TILE, axis=-1)


def reference(factor, diag_inverse, parent, tile_node, structure):
    reach = ancestors(parent)
    node_hot = (tile_node[:, :, None] == jnp.arange(M, dtype=jnp.int32)[None, None, :]).astype(jnp.float32)
    high = lax.Precision.HIGHEST
    tile_above = jnp.einsum('rta,ba,cub->rtcu', node_hot, reach, node_hot, precision=high)
    tile_same = jnp.einsum('rta,cua->rtcu', node_hot, node_hot, precision=high)
    tile_struct = jnp.einsum('cub,brt->rtcu', node_hot, structure.astype(jnp.float32), precision=high)
    sigma_all = jnp.zeros((LEV, NL, LEV, NL), jnp.float32)
    root_mask = spread_both(tile_same[0, :, 0, :])
    sigma_all = sigma_all.at[0, :, 0, :].set(root_mask * diag_inverse[0])
    for level_no in range(1, LEV):
        width = level_no * NL
        known_bf = sigma_all[:level_no, :, :level_no, :].reshape(width, width).astype(jnp.bfloat16)
        struct_mask = spread_both(tile_struct[:level_no, :, level_no, :]).astype(jnp.bfloat16)
        panel_mat = (factor[:level_no, :, level_no, :] * struct_mask).reshape(width, NL)
        above_mask = spread_both(tile_above[:level_no, :, level_no, :]).reshape(width, NL)
        column = -(jnp.dot(known_bf, panel_mat, preferred_element_type=jnp.float32) * above_mask)
        sigma_all = sigma_all.at[:level_no, :, level_no, :].set(column.reshape(level_no, NL, NL))
        mirror = column.T
        sigma_all = sigma_all.at[level_no, :, :level_no, :].set(mirror.reshape(NL, level_no, NL))
        inner_sum = jnp.dot(mirror.astype(jnp.bfloat16), panel_mat, preferred_element_type=jnp.float32)
        same_mask = spread_both(tile_same[level_no, :, level_no, :])
        sigma_all = sigma_all.at[level_no, :, level_no, :].set(same_mask * (diag_inverse[level_no] - inner_sum))
    return sigma_all
```

```python
import jax
import jax.numpy as jnp
from jax import lax
from jax.sharding import PartitionSpec as P

LEV = 4
TILE = 256
LT = 8
M = 15
BF = jnp.bfloat16
F32 = jnp.float32


def ancestors(parent):
    node_ids = jnp.arange(M, dtype=jnp.int32)
    step_mat = (parent[:, None] == node_ids[None, :]).astype(jnp.float32)
    power_mat = step_mat
    reach = step_mat
    for hop_count in range(LEV - 2):
        power_mat = jnp.dot(power_mat, step_mat, precision=lax.Precision.HIGHEST)
        reach = reach + power_mat
    return reach


def spread(mask_tile):
    return jnp.repeat(mask_tile, TILE, axis=-1)


def narrow_all(x, axis):
    size = lax.axis_size("narrow")
    mine = lax.axis_index("narrow")
    if size == 2:
        other = lax.ppermute(x, "narrow", [(0, 1), (1, 0)])
        first = mine == 0
        return jnp.concatenate([jnp.where(first, x, other), jnp.where(first, other, x)], axis=axis)
    shape = list(x.shape)
    width = shape[axis]
    shape[axis] = width * size
    out = jnp.zeros(shape, x.dtype)
    for hop in range(size):
        got = x if hop == 0 else lax.ppermute(x, "narrow", [(i, (i + hop) % size) for i in range(size)])
        out = lax.dynamic_update_slice_in_dim(out, got, (mine - hop) % size * width, axis)
    return out


def wide_all(x):
    wide = lax.axis_size("wide")
    narrow = lax.axis_size("narrow")
    row_id = lax.axis_index("wide")
    depth = wide // 4
    z, y_id, x_id = row_id // 4, row_id // 2 % 2, row_id % 2
    l, r, c = x.shape
    line = jnp.zeros((l, depth, r, c), x.dtype)
    for hop in range(depth):
        got = x
        if hop:
            got = lax.ppermute(x, "wide", [(i, (i + 4 * hop) % wide) for i in range(wide)])
        line = lax.dynamic_update_slice(line, got[:, None], (0, (z - hop) % depth, 0, 0))

    def swap(value, turn):
        pairs = []
        for i in range(wide):
            for j in range(narrow):
                pairs.append((i * narrow + j, (i ^ (1 if (j + turn) % 2 == 0 else 2)) * narrow + j))
        return lax.ppermute(value, ("wide", "narrow"), pairs)

    even = lax.axis_index("narrow") % 2 == 0
    near = swap(line, 0)
    far = swap(jnp.stack([line, near]), 1)
    out = jnp.zeros((l, depth, 2, 2, r, c), x.dtype)
    near_y, near_x = jnp.where(even, y_id, 1 - y_id), jnp.where(even, 1 - x_id, x_id)
    far_y, far_x = jnp.where(even, 1 - y_id, y_id), jnp.where(even, x_id, 1 - x_id)
    for piece, yy, xx in (
        (line, y_id, x_id),
        (near, near_y, near_x),
        (far[0], far_y, far_x),
        (far[1], 1 - y_id, 1 - x_id),
    ):
        out = lax.dynamic_update_slice(out, piece[:, :, None, None], (0, 0, yy, xx, 0, 0))
    return out.reshape(l, wide * r, c)


def mirrored(full):
    wide = lax.axis_size("wide")
    narrow = lax.axis_size("narrow")
    l, r, cols = full.shape
    part = r // narrow
    mine = lax.dynamic_slice_in_dim(full, lax.axis_index("narrow") * part, part, 1)
    slots = mine.reshape(l, part, wide, r).transpose(2, 0, 1, 3)
    got = lax.all_to_all(slots, "wide", split_axis=0, concat_axis=0, tiled=True)
    whole = narrow_all(got, 2)
    return whole.transpose(3, 1, 0, 2).reshape(r, l, cols)


def local(factor, diag_inverse, parent, tile_node, structure):
    row_count = factor.shape[1]
    col_count = factor.shape[3]
    col_tiles = col_count // TILE
    row_id = lax.axis_index("wide")
    col_id = lax.axis_index("narrow")
    high = lax.Precision.HIGHEST
    reach = ancestors(parent)
    node_hot = (tile_node[:, :, None] == jnp.arange(M, dtype=jnp.int32)[None, None, :]).astype(
        jnp.float32
    )
    row_pos = row_id * row_count // TILE
    pos_hot = (jnp.arange(LT, dtype=jnp.int32) == row_pos).astype(jnp.float32)
    row_hot = jnp.einsum("t,ltm->lm", pos_hot, node_hot, precision=high)
    col_sel = (
        jnp.arange(LT, dtype=jnp.int32)[None, :]
        == (col_id * col_tiles + jnp.arange(col_tiles, dtype=jnp.int32))[:, None]
    ).astype(jnp.float32)
    col_hot = jnp.einsum("jt,ltm->ljm", col_sel, node_hot, precision=high)
    tile_above = jnp.einsum("ra,ba,cjb->rcj", row_hot, reach, col_hot, precision=high)
    tile_same = jnp.einsum("lm,ljm->lj", row_hot, col_hot, precision=high)
    struct_row = jnp.einsum("mlt,t->ml", structure.astype(jnp.float32), pos_hot, precision=high)
    tile_struct = jnp.einsum("cjm,mr->rcj", col_hot, struct_row, precision=high)

    panels = {}
    for level in range(1, LEV):
        mask = spread(tile_struct[:level, level])[:, None, :].astype(BF)
        panels[level] = wide_all(factor[:level, :, level, :] * mask)

    blocks = {(0, 0): spread(tile_same[0])[None, :] * diag_inverse[0]}
    rows = {0: [narrow_all(blocks[0, 0].astype(BF), 1)]}
    for level in range(1, LEV):
        panel = panels[level].reshape(level * LT * TILE, col_count)
        known = jnp.concatenate([jnp.concatenate(rows[k], axis=1) for k in range(level)], axis=0)
        product = jnp.dot(known, panel, preferred_element_type=F32)
        above = spread(tile_above[:level, level])[:, None, :]
        column = -(product.reshape(level, row_count, col_count) * above)
        for k in range(level):
            blocks[k, level] = column[k]
        full = narrow_all(column.astype(BF), 2)
        for k in range(level):
            rows[k].append(full[k])
        mirror = mirrored(full)
        here = lax.dynamic_slice_in_dim(mirror, col_id * col_count, col_count, 2).astype(F32)
        for k in range(level):
            blocks[level, k] = here[:, k]
        inner = jnp.dot(
            mirror.reshape(row_count, level * LT * TILE), panel, preferred_element_type=F32
        )
        blocks[level, level] = spread(tile_same[level])[None, :] * (diag_inverse[level] - inner)
        if level < LEV - 1:
            rows[level] = [mirror[:, k] for k in range(level)]
            rows[level].append(narrow_all(blocks[level, level].astype(BF), 1))
    return jnp.stack(
        [jnp.stack([blocks[k, m] for m in range(LEV)], axis=1) for k in range(LEV)], axis=0
    )


def solution(mesh):
    return jax.shard_map(
        local,
        mesh=mesh,
        in_specs=(P(None, "wide", None, "narrow"), P(None, "wide", "narrow"), P(), P(), P()),
        out_specs=P(None, "wide", None, "narrow"),
        check_vma=False,
    )
```

```python
import functools

import jax
import jax.numpy as jnp
from jax import lax
from jax.experimental import pallas as pl
from jax.experimental.pallas import tpu as pltpu
from jax.sharding import PartitionSpec as P

LEV = 4
TILE = 256
LT = 8
M = 15
BF = jnp.bfloat16
F32 = jnp.float32
VMEM = 56 * 1024 * 1024


def ancestors(parent):
    node_ids = jnp.arange(M, dtype=jnp.int32)
    step_mat = (parent[:, None] == node_ids[None, :]).astype(jnp.float32)
    power_mat = step_mat
    reach = step_mat
    for hop_count in range(LEV - 2):
        power_mat = jnp.dot(power_mat, step_mat, precision=lax.Precision.HIGHEST)
        reach = reach + power_mat
    return reach


def spread(mask_tile):
    return jnp.repeat(mask_tile, TILE, axis=-1)


def after(value, *others):
    return lax.optimization_barrier((value,) + others)[0]


def narrow_all(x, axis):
    size = lax.axis_size("narrow")
    mine = lax.axis_index("narrow")
    if size == 2:
        other = lax.ppermute(x, "narrow", [(0, 1), (1, 0)])
        first = mine == 0
        return jnp.concatenate([jnp.where(first, x, other), jnp.where(first, other, x)], axis=axis)
    shape = list(x.shape)
    width = shape[axis]
    shape[axis] = width * size
    out = jnp.zeros(shape, x.dtype)
    for hop in range(size):
        got = x if hop == 0 else lax.ppermute(x, "narrow", [(i, (i + hop) % size) for i in range(size)])
        out = lax.dynamic_update_slice_in_dim(out, got, (mine - hop) % size * width, axis)
    return out


def swap(value, turn):
    wide = lax.axis_size("wide")
    narrow = lax.axis_size("narrow")
    pairs = []
    for i in range(wide):
        for j in range(narrow):
            pairs.append((i * narrow + j, (i ^ (1 if (j + turn) % 2 == 0 else 2)) * narrow + j))
    return lax.ppermute(value, ("wide", "narrow"), pairs)


def shifts(value):
    wide = lax.axis_size("wide")
    return [value] + [
        lax.ppermute(value, "wide", [(i, (i + 4 * hop) % wide) for i in range(wide)])
        for hop in range(1, wide // 4)
    ]


def positions(z_last):
    wide = lax.axis_size("wide")
    depth = wide // 4
    row_id = lax.axis_index("wide")
    odd = lax.axis_index("narrow") % 2
    z = (row_id // 4 - jnp.arange(depth, dtype=jnp.int32)) % depth
    flips = jnp.stack([0 * odd, 1 + odd, 2 - odd, 3 + 0 * odd])
    near = (row_id % 4) ^ flips
    if z_last:
        return (z[:, None] * 4 + near[None, :]).reshape(-1).astype(jnp.int32)
    return (z[None, :] * 4 + near[:, None]).reshape(-1).astype(jnp.int32)


def along_z(x, gate):
    return shifts(x if gate is None else after(x, gate))


def along_xy(pieces, gate):
    if gate is not None:
        held = lax.optimization_barrier(tuple(pieces) + (gate,))
        pieces = held[:-1]
    line = jnp.stack(pieces)
    return [line, swap(line, 0), swap(line, 1)]


def along_both(arrays, gate):
    near = arrays[1]
    return arrays + [swap(near if gate is None else after(near, gate), 1)]


def product_body(plan, rows_n, steps_n, finish, *refs):
    place_ref, mask_ref = refs[0], refs[1]
    refs = refs[2:]
    row_refs = [refs[q * steps_n : (q + 1) * steps_n] for q in range(rows_n)]
    refs = refs[rows_n * steps_n :]
    count = sum(arrays for _, arrays, _ in plan)
    piece_refs, refs = refs[:count], refs[count:]
    if finish:
        diag_ref, out_ref, low_ref, lhs = refs
    else:
        out_ref, lhs = refs
    r = row_refs[0][0].shape[0]
    width = piece_refs[0].shape[-1]

    @pl.when(pl.program_id(0) == 0)
    def _():
        at = 0
        for g, (levels, arrays, each) in enumerate(plan):
            for i in range(arrays * each):
                start = pl.multiple_of(place_ref[g, i] * r, r)
                for j in levels:
                    for q in range(rows_n):
                        lhs[q * r : (q + 1) * r, at : at + r] = row_refs[q][j][:, pl.ds(start, r)]
                    at += r

    total = None
    at, base = 0, 0
    for levels, arrays, each in plan:
        depth = each * len(levels) * r
        for a in range(arrays):
            part = jnp.dot(
                lhs[:, at : at + depth],
                piece_refs[base + a][...].reshape(depth, width),
                preferred_element_type=F32,
            )
            total = part if total is None else total + part
            at += depth
        base += arrays
    here = pl.program_id(0)
    for q in range(rows_n):
        for t in range(width // TILE):
            keep = mask_ref[q, here * (width // TILE) + t] > 0
            cols = slice(t * TILE, (t + 1) * TILE)
            value = total[q * r : (q + 1) * r, cols]
            if finish:
                value = diag_ref[0, :, cols] - value
            else:
                value = -value
            value = jnp.where(keep, value, 0.0)
            if finish:
                out_ref[:, cols] = value
                low_ref[:, cols] = value.astype(BF)
            else:
                out_ref[q, :, cols] = value.astype(BF)


def product(rows, groups, mask, diag=None, shift=0):
    r = rows[0][0].shape[0]
    c = groups[0][2][0].shape[-1]
    rows_n, steps_n = len(rows), len(rows[0])
    if r % 128:
        total = 0.0
        for levels, place, arrays in groups:
            at = 0
            for array in arrays:
                each = array.shape[0]
                here = place[at : at + each]
                lhs = jnp.concatenate(
                    [
                        jnp.stack(
                            [jnp.take(row[j].reshape(r, -1, r), here, axis=1) for j in levels], axis=2
                        ).reshape(r, -1)
                        for row in rows
                    ],
                    axis=0,
                )
                total += jnp.dot(lhs, array.reshape(-1, c), preferred_element_type=F32)
                at += each
        total = total.reshape(rows_n, r, c)
        keep = jnp.repeat(mask, TILE, axis=1)[:, None, :] > 0
        if diag is None:
            return jnp.where(keep, -total, 0.0).astype(BF)
        level = diag[1]
        value = jnp.where(keep[0], diag[0][level, :, shift : shift + c] - total[0], 0.0)
        return value, value.astype(BF)
    width = TILE
    plan = tuple((tuple(levels), len(arrays), arrays[0].shape[0]) for levels, _, arrays in groups)
    place = jnp.stack([p for _, p, _ in groups])
    whole = pl.BlockSpec(memory_space=pltpu.VMEM)
    scalar = pl.BlockSpec(memory_space=pltpu.SMEM)
    pieces = [a for _, _, arrays in groups for a in arrays]
    piece_specs = [pl.BlockSpec(a.shape[:3] + (width,), lambda i: (0, 0, 0, i)) for a in pieces]
    flat = [x for row in rows for x in row]
    operands = [place, mask] + flat + pieces
    specs = [scalar, scalar] + [whole] * len(flat) + piece_specs
    if diag is None:
        outs = jax.ShapeDtypeStruct((rows_n, r, c), BF)
        out_specs = pl.BlockSpec((rows_n, r, width), lambda i: (0, 0, i))
    else:
        level = diag[1]
        skip = shift // width
        operands.append(diag[0])
        specs.append(pl.BlockSpec((1, r, width), lambda i: (level, 0, skip + i)))
        outs = (jax.ShapeDtypeStruct((r, c), F32), jax.ShapeDtypeStruct((r, c), BF))
        out_specs = (pl.BlockSpec((r, width), lambda i: (0, i)),) * 2
    deep = sum(len(levels) * arrays * each for levels, arrays, each in plan) * r
    return pl.pallas_call(
        functools.partial(product_body, plan, rows_n, steps_n, diag is not None),
        grid=(c // width,),
        in_specs=specs,
        out_specs=out_specs,
        out_shape=outs,
        scratch_shapes=[pltpu.VMEM((rows_n * r, deep), BF)],
        compiler_params=pltpu.CompilerParams(vmem_limit_bytes=VMEM),
        cost_estimate=pl.CostEstimate(
            flops=1, bytes_accessed=1, transcendentals=0
        ),
    )(*operands)


def slots_body(levels, wide, id_ref, own_ref, other_ref, slots_ref, full_ref):
    r, c = own_ref.shape[1:]
    part = r // 2
    half = wide // 2
    for n in range(2):

        @pl.when(id_ref[0] == n)
        def _():
            for h in range(2):
                ref = own_ref if h == n else other_ref
                for k in range(levels):
                    full_ref[k, :, h * c : (h + 1) * c] = ref[k]
                    for i in range(half):
                        slots_ref[h * half + i, k] = ref[k, n * part : (n + 1) * part, i * r : (i + 1) * r]


def make_slots(value):
    wide = lax.axis_size("wide")
    narrow = lax.axis_size("narrow")
    l, r, c = value.shape
    if narrow != 2 or r % 128:
        full = narrow_all(value, 2)
        part = r // narrow
        mine = lax.dynamic_slice_in_dim(full, lax.axis_index("narrow") * part, part, 1)
        return mine.reshape(l, part, wide, r).transpose(2, 0, 1, 3), full
    other = lax.ppermute(value, "narrow", [(0, 1), (1, 0)])
    whole = pl.BlockSpec(memory_space=pltpu.VMEM)
    return pl.pallas_call(
        functools.partial(slots_body, l, wide),
        in_specs=[pl.BlockSpec(memory_space=pltpu.SMEM), whole, whole],
        out_specs=(whole, whole),
        out_shape=(
            jax.ShapeDtypeStruct((wide, l, r // 2, r), BF),
            jax.ShapeDtypeStruct((l, r, 2 * c), BF),
        ),
        compiler_params=pltpu.CompilerParams(vmem_limit_bytes=VMEM),
        cost_estimate=pl.CostEstimate(flops=1, bytes_accessed=1, transcendentals=0),
    )(lax.axis_index("narrow").astype(jnp.int32).reshape(1), value, other)


def turn_body(levels, wide, id_ref, own_ref, other_ref, out_ref):
    r = out_ref.shape[1]
    for n in range(2):

        @pl.when(id_ref[0] == n)
        def _():
            first, second = (own_ref, other_ref) if n == 0 else (other_ref, own_ref)
            for k in range(levels):
                for w in range(wide):
                    block = jnp.concatenate([first[w, k], second[w, k]], axis=0)
                    out_ref[k, :, w * r : (w + 1) * r] = block.T


def mirrored(got, full):
    wide = lax.axis_size("wide")
    narrow = lax.axis_size("narrow")
    l, r, cols = full.shape
    if narrow != 2 or r % 128:
        return narrow_all(got, 2).transpose(1, 3, 0, 2).reshape(l, r, cols)
    other = lax.ppermute(got, "narrow", [(0, 1), (1, 0)])
    whole = pl.BlockSpec(memory_space=pltpu.VMEM)
    return pl.pallas_call(
        functools.partial(turn_body, l, wide),
        in_specs=[pl.BlockSpec(memory_space=pltpu.SMEM), whole, whole],
        out_specs=whole,
        out_shape=jax.ShapeDtypeStruct((l, r, cols), BF),
        compiler_params=pltpu.CompilerParams(vmem_limit_bytes=VMEM),
        cost_estimate=pl.CostEstimate(flops=1, bytes_accessed=1, transcendentals=0),
    )(lax.axis_index("narrow").astype(jnp.int32).reshape(1), got, other)


def upper_body(id_ref, first_ref, *refs):
    news, turns, diags, out_ref = refs[0:3], refs[3:5], refs[5:7], refs[7]
    for k in range(LEV - 1):
        for m in range(LEV):
            if m == k:
                value = first_ref[0] if k == 0 else diags[k - 1][...]
            elif m > k:
                value = news[m - 1][k].astype(F32)
            else:
                value = turns[k - 1][m].astype(F32)
            out_ref[k, :, m, :] = value


def lower_body(id_ref, turn_ref, diag_ref, held_ref, out_ref):
    for m in range(LEV - 1):
        out_ref[0, :, m, :] = turn_ref[m].astype(F32)
    out_ref[0, :, LEV - 1, :] = diag_ref[...]


def upper_rows(diag_inverse, news, turns, diags):
    r, c = diag_inverse.shape[1:]
    step = min(r, 32)
    shape = jax.ShapeDtypeStruct((LEV, r, LEV, c), F32)
    specs = [pl.BlockSpec((1, step, c), lambda i, n: (0, i, 0))]
    specs += [pl.BlockSpec((m, step, c), lambda i, n: (0, i, 0)) for m in range(1, LEV)]
    specs += [pl.BlockSpec((k, step, c), lambda i, n: (0, i, n[0])) for k in range(1, LEV - 1)]
    specs += [pl.BlockSpec((step, c), lambda i, n: (i, 0)) for k in range(1, LEV - 1)]
    return pl.pallas_call(
        upper_body,
        grid_spec=pltpu.PrefetchScalarGridSpec(
            num_scalar_prefetch=1,
            grid=(r // step,),
            in_specs=specs,
            out_specs=pl.BlockSpec((LEV - 1, step, LEV, c), lambda i, n: (0, i, 0, 0)),
        ),
        out_shape=shape,
        compiler_params=pltpu.CompilerParams(vmem_limit_bytes=VMEM),
        cost_estimate=pl.CostEstimate(flops=0, bytes_accessed=1, transcendentals=0),
    )(lax.axis_index("narrow").astype(jnp.int32).reshape(1), diag_inverse, *news, *turns, *diags)


def lower_rows(turn, diag, held):
    r, c = diag.shape
    step = min(r, 32)
    return pl.pallas_call(
        lower_body,
        grid_spec=pltpu.PrefetchScalarGridSpec(
            num_scalar_prefetch=1,
            grid=(r // step,),
            in_specs=[
                pl.BlockSpec((LEV - 1, step, c), lambda i, n: (0, i, n[0])),
                pl.BlockSpec((step, c), lambda i, n: (i, 0)),
                pl.BlockSpec(memory_space=pl.ANY),
            ],
            out_specs=pl.BlockSpec((1, step, LEV, c), lambda i, n: (LEV - 1, i, 0, 0)),
        ),
        out_shape=jax.ShapeDtypeStruct(held.shape, F32),
        input_output_aliases={3: 0},
        compiler_params=pltpu.CompilerParams(vmem_limit_bytes=VMEM),
        cost_estimate=pl.CostEstimate(flops=0, bytes_accessed=1, transcendentals=0),
    )(lax.axis_index("narrow").astype(jnp.int32).reshape(1), turn, diag, held)


def local(factor, diag_inverse, parent, tile_node, structure):
    row_count = factor.shape[1]
    col_count = factor.shape[3]
    col_tiles = col_count // TILE
    row_id = lax.axis_index("wide")
    col_id = lax.axis_index("narrow")
    high = lax.Precision.HIGHEST
    reach = ancestors(parent)
    node_hot = (tile_node[:, :, None] == jnp.arange(M, dtype=jnp.int32)[None, None, :]).astype(
        jnp.float32
    )
    row_pos = row_id * row_count // TILE
    pos_hot = (jnp.arange(LT, dtype=jnp.int32) == row_pos).astype(jnp.float32)
    row_hot = jnp.einsum("t,ltm->lm", pos_hot, node_hot, precision=high)
    col_sel = (
        jnp.arange(LT, dtype=jnp.int32)[None, :]
        == (col_id * col_tiles + jnp.arange(col_tiles, dtype=jnp.int32))[:, None]
    ).astype(jnp.float32)
    col_hot = jnp.einsum("jt,ltm->ljm", col_sel, node_hot, precision=high)
    tile_above = jnp.einsum("ra,ba,cjb->rcj", row_hot, reach, col_hot, precision=high)
    tile_same = jnp.einsum("lm,ljm->lj", row_hot, col_hot, precision=high)
    struct_row = jnp.einsum("mlt,t->ml", structure.astype(jnp.float32), pos_hot, precision=high)
    tile_struct = jnp.einsum("cjm,mr->rcj", col_hot, struct_row, precision=high)
    above = (tile_above > 0.5).astype(jnp.int32)
    same = (tile_same > 0.5).astype(jnp.int32)

    def masked(k, m):
        return (factor[k, :, m, :] * spread(tile_struct[k, m])[None, :].astype(BF))[None]

    place = positions(False)

    def panel_of(level):
        return jnp.concatenate([masked(k, level) for k in range(level)], axis=0)

    wide = lax.axis_size("wide")
    whole_place = jnp.arange(wide, dtype=jnp.int32)
    last = lax.all_gather(panel_of(3), "wide", axis=0)
    first = along_z(panel_of(1), None)
    gathered_two = lax.all_gather(panel_of(2), "wide", axis=0)
    gathered = {1: along_both(along_xy(first, None), None)}
    gathered[3] = [last]
    gathered[2] = [gathered_two]

    rows = {0: [narrow_all(diag_inverse[0].astype(BF), 1)]}
    news, turns, diags = [], [], []
    for level in range(1, LEV):
        arrays = gathered[level]
        known = [rows[k] for k in range(level)]
        groups = [(tuple(range(level)), place if level == 1 else whole_place, arrays)]
        value = product(known, groups, above[:level, level])
        news.append(value)
        if level == 1:
            pass
        slots, full = make_slots(value)
        for k in range(level):
            rows[k].append(full[k])
        if level == LEV - 1:
            out = upper_rows(diag_inverse, news, turns, diags)
        got = lax.all_to_all(slots, "wide", split_axis=0, concat_axis=0, tiled=True)
        turn = mirrored(got, full)
        turns.append(turn)
        rows[level] = [turn[k] for k in range(level)]
        done, low = product([rows[level]], groups, same[level : level + 1], (diag_inverse, level))
        diags.append(done)
        if level < LEV - 1:
            rows[level].append(narrow_all(low, 1))
    return lower_rows(turns[-1], diags[-1], out)


def solution(mesh):
    return jax.shard_map(
        local,
        mesh=mesh,
        in_specs=(P(None, "wide", None, "narrow"), P(None, "wide", "narrow"), P(), P(), P()),
        out_specs=P(None, "wide", None, "narrow"),
        check_vma=False,
    )
```

```python
import functools

import jax
import jax.numpy as jnp
from jax import lax
from jax.experimental import pallas as pl
from jax.experimental.pallas import tpu as pltpu
from jax.sharding import PartitionSpec as P

LEV = 4
TILE = 256
LT = 8
M = 15
BF = jnp.bfloat16
F32 = jnp.float32
VMEM = 56 * 1024 * 1024


def ancestors(parent):
    node_ids = jnp.arange(M, dtype=jnp.int32)
    step_mat = (parent[:, None] == node_ids[None, :]).astype(jnp.float32)
    power_mat = step_mat
    reach = step_mat
    for hop_count in range(LEV - 2):
        power_mat = jnp.dot(power_mat, step_mat, precision=lax.Precision.HIGHEST)
        reach = reach + power_mat
    return reach


def spread(mask_tile):
    return jnp.repeat(mask_tile, TILE, axis=-1)


def after(value, *others):
    return lax.optimization_barrier((value,) + others)[0]


def narrow_all(x, axis):
    size = lax.axis_size("narrow")
    mine = lax.axis_index("narrow")
    if size == 2:
        other = lax.ppermute(x, "narrow", [(0, 1), (1, 0)])
        first = mine == 0
        return jnp.concatenate([jnp.where(first, x, other), jnp.where(first, other, x)], axis=axis)
    shape = list(x.shape)
    width = shape[axis]
    shape[axis] = width * size
    out = jnp.zeros(shape, x.dtype)
    for hop in range(size):
        got = x if hop == 0 else lax.ppermute(x, "narrow", [(i, (i + hop) % size) for i in range(size)])
        out = lax.dynamic_update_slice_in_dim(out, got, (mine - hop) % size * width, axis)
    return out


def swap(value, turn):
    wide = lax.axis_size("wide")
    narrow = lax.axis_size("narrow")
    pairs = []
    for i in range(wide):
        for j in range(narrow):
            pairs.append((i * narrow + j, (i ^ (1 if (j + turn) % 2 == 0 else 2)) * narrow + j))
    return lax.ppermute(value, ("wide", "narrow"), pairs)


def shifts(value):
    wide = lax.axis_size("wide")
    return [value] + [
        lax.ppermute(value, "wide", [(i, (i + 4 * hop) % wide) for i in range(wide)])
        for hop in range(1, wide // 4)
    ]


def positions(z_last):
    wide = lax.axis_size("wide")
    depth = wide // 4
    row_id = lax.axis_index("wide")
    odd = lax.axis_index("narrow") % 2
    z = (row_id // 4 - jnp.arange(depth, dtype=jnp.int32)) % depth
    flips = jnp.stack([0 * odd, 1 + odd, 2 - odd, 3 + 0 * odd])
    near = (row_id % 4) ^ flips
    if z_last:
        return (z[:, None] * 4 + near[None, :]).reshape(-1).astype(jnp.int32)
    return (z[None, :] * 4 + near[:, None]).reshape(-1).astype(jnp.int32)


def along_z(x, gate):
    return shifts(x if gate is None else after(x, gate))


def along_xy(pieces, gate):
    if gate is not None:
        held = lax.optimization_barrier(tuple(pieces) + (gate,))
        pieces = held[:-1]
    line = jnp.stack(pieces)
    return [line, swap(line, 0), swap(line, 1)]


def along_both(arrays, gate):
    near = arrays[1]
    return arrays + [swap(near if gate is None else after(near, gate), 1)]


def product_body(plan, rows_n, steps_n, finish, *refs):
    place_ref, mask_ref = refs[0], refs[1]
    refs = refs[2:]
    row_refs = [refs[q * steps_n : (q + 1) * steps_n] for q in range(rows_n)]
    refs = refs[rows_n * steps_n :]
    count = sum(arrays for _, arrays, _ in plan)
    piece_refs, refs = refs[:count], refs[count:]
    if finish:
        diag_ref, out_ref, low_ref, lhs = refs
    else:
        out_ref, lhs = refs
    r = row_refs[0][0].shape[0]
    width = piece_refs[0].shape[-1]

    @pl.when(pl.program_id(0) == 0)
    def _():
        at = 0
        for g, (levels, arrays, each) in enumerate(plan):
            for i in range(arrays * each):
                start = pl.multiple_of(place_ref[g, i] * r, r)
                for j in levels:
                    for q in range(rows_n):
                        lhs[q * r : (q + 1) * r, at : at + r] = row_refs[q][j][:, pl.ds(start, r)]
                    at += r

    total = None
    at, base = 0, 0
    for levels, arrays, each in plan:
        depth = each * len(levels) * r
        for a in range(arrays):
            part = jnp.dot(
                lhs[:, at : at + depth],
                piece_refs[base + a][...].reshape(depth, width),
                preferred_element_type=F32,
            )
            total = part if total is None else total + part
            at += depth
        base += arrays
    here = pl.program_id(0)
    for q in range(rows_n):
        for t in range(width // TILE):
            keep = mask_ref[q, here * (width // TILE) + t] > 0
            cols = slice(t * TILE, (t + 1) * TILE)
            value = total[q * r : (q + 1) * r, cols]
            if finish:
                value = diag_ref[0, :, cols] - value
            else:
                value = -value
            value = jnp.where(keep, value, 0.0)
            if finish:
                out_ref[:, cols] = value
                low_ref[:, cols] = value.astype(BF)
            else:
                out_ref[q, :, cols] = value.astype(BF)


def product(rows, groups, mask, diag=None, shift=0):
    r = rows[0][0].shape[0]
    c = groups[0][2][0].shape[-1]
    rows_n, steps_n = len(rows), len(rows[0])
    if r % 128:
        total = 0.0
        for levels, place, arrays in groups:
            at = 0
            for array in arrays:
                each = array.shape[0]
                here = place[at : at + each]
                lhs = jnp.concatenate(
                    [
                        jnp.stack(
                            [jnp.take(row[j].reshape(r, -1, r), here, axis=1) for j in levels], axis=2
                        ).reshape(r, -1)
                        for row in rows
                    ],
                    axis=0,
                )
                total += jnp.dot(lhs, array.reshape(-1, c), preferred_element_type=F32)
                at += each
        total = total.reshape(rows_n, r, c)
        keep = jnp.repeat(mask, TILE, axis=1)[:, None, :] > 0
        if diag is None:
            return jnp.where(keep, -total, 0.0).astype(BF)
        level = diag[1]
        value = jnp.where(keep[0], diag[0][level, :, shift : shift + c] - total[0], 0.0)
        return value, value.astype(BF)
    width = TILE
    plan = tuple((tuple(levels), len(arrays), arrays[0].shape[0]) for levels, _, arrays in groups)
    place = jnp.stack([p for _, p, _ in groups])
    whole = pl.BlockSpec(memory_space=pltpu.VMEM)
    scalar = pl.BlockSpec(memory_space=pltpu.SMEM)
    pieces = [a for _, _, arrays in groups for a in arrays]
    piece_specs = [pl.BlockSpec(a.shape[:3] + (width,), lambda i: (0, 0, 0, i)) for a in pieces]
    flat = [x for row in rows for x in row]
    operands = [place, mask] + flat + pieces
    specs = [scalar, scalar] + [whole] * len(flat) + piece_specs
    if diag is None:
        outs = jax.ShapeDtypeStruct((rows_n, r, c), BF)
        out_specs = pl.BlockSpec((rows_n, r, width), lambda i: (0, 0, i))
    else:
        level = diag[1]
        skip = shift // width
        operands.append(diag[0])
        specs.append(pl.BlockSpec((1, r, width), lambda i: (level, 0, skip + i)))
        outs = (jax.ShapeDtypeStruct((r, c), F32), jax.ShapeDtypeStruct((r, c), BF))
        out_specs = (pl.BlockSpec((r, width), lambda i: (0, i)),) * 2
    deep = sum(len(levels) * arrays * each for levels, arrays, each in plan) * r
    return pl.pallas_call(
        functools.partial(product_body, plan, rows_n, steps_n, diag is not None),
        grid=(c // width,),
        in_specs=specs,
        out_specs=out_specs,
        out_shape=outs,
        scratch_shapes=[pltpu.VMEM((rows_n * r, deep), BF)],
        compiler_params=pltpu.CompilerParams(vmem_limit_bytes=VMEM),
        cost_estimate=pl.CostEstimate(
            flops=1, bytes_accessed=1, transcendentals=0
        ),
    )(*operands)


def slots_body(levels, wide, id_ref, own_ref, other_ref, slots_ref, full_ref):
    r, c = own_ref.shape[1:]
    part = r // 2
    half = wide // 2
    for n in range(2):

        @pl.when(id_ref[0] == n)
        def _():
            for h in range(2):
                ref = own_ref if h == n else other_ref
                for k in range(levels):
                    full_ref[k, :, h * c : (h + 1) * c] = ref[k]
                    for i in range(half):
                        slots_ref[h * half + i, k] = ref[k, n * part : (n + 1) * part, i * r : (i + 1) * r]


def make_slots(value):
    wide = lax.axis_size("wide")
    narrow = lax.axis_size("narrow")
    l, r, c = value.shape
    if narrow != 2 or r % 128:
        full = narrow_all(value, 2)
        part = r // narrow
        mine = lax.dynamic_slice_in_dim(full, lax.axis_index("narrow") * part, part, 1)
        return mine.reshape(l, part, wide, r).transpose(2, 0, 1, 3), full
    other = lax.ppermute(value, "narrow", [(0, 1), (1, 0)])
    whole = pl.BlockSpec(memory_space=pltpu.VMEM)
    return pl.pallas_call(
        functools.partial(slots_body, l, wide),
        in_specs=[pl.BlockSpec(memory_space=pltpu.SMEM), whole, whole],
        out_specs=(whole, whole),
        out_shape=(
            jax.ShapeDtypeStruct((wide, l, r // 2, r), BF),
            jax.ShapeDtypeStruct((l, r, 2 * c), BF),
        ),
        compiler_params=pltpu.CompilerParams(vmem_limit_bytes=VMEM),
        cost_estimate=pl.CostEstimate(flops=1, bytes_accessed=1, transcendentals=0),
    )(lax.axis_index("narrow").astype(jnp.int32).reshape(1), value, other)


def turn_body(levels, wide, id_ref, own_ref, other_ref, out_ref):
    r = out_ref.shape[1]
    for n in range(2):

        @pl.when(id_ref[0] == n)
        def _():
            first, second = (own_ref, other_ref) if n == 0 else (other_ref, own_ref)
            for k in range(levels):
                for w in range(wide):
                    block = jnp.concatenate([first[w, k], second[w, k]], axis=0)
                    out_ref[k, :, w * r : (w + 1) * r] = block.T


def mirrored(got, full):
    wide = lax.axis_size("wide")
    narrow = lax.axis_size("narrow")
    l, r, cols = full.shape
    if narrow != 2 or r % 128:
        return narrow_all(got, 2).transpose(1, 3, 0, 2).reshape(l, r, cols)
    other = lax.ppermute(got, "narrow", [(0, 1), (1, 0)])
    whole = pl.BlockSpec(memory_space=pltpu.VMEM)
    return pl.pallas_call(
        functools.partial(turn_body, l, wide),
        in_specs=[pl.BlockSpec(memory_space=pltpu.SMEM), whole, whole],
        out_specs=whole,
        out_shape=jax.ShapeDtypeStruct((l, r, cols), BF),
        compiler_params=pltpu.CompilerParams(vmem_limit_bytes=VMEM),
        cost_estimate=pl.CostEstimate(flops=1, bytes_accessed=1, transcendentals=0),
    )(lax.axis_index("narrow").astype(jnp.int32).reshape(1), got, other)


SRC, POS, HELD, OWN, KEEP = 0, 16, 24, 40, 48
WIDTHS = {2: (4, 2), 3: (4, 2, 1)}


def table_body(id_ref, parent_ref, node_ref, structure_ref, out_ref):
    core, row = id_ref[0], id_ref[1]
    for i in range(out_ref.shape[0]):
        out_ref[i] = jnp.int32(0)
    one, none = jnp.int32(1), jnp.int32(0)
    nodes = [[node_ref[k, t] for t in range(LT)] for k in range(LEV)]
    above = [[parent_ref[nodes[k][t]] for t in range(LT)] for k in range(LEV)]
    left = nodes[1][0]
    key1 = [jnp.where(nodes[1][t] == left, none, one) for t in range(LT)]

    def second(k, t):
        found = none
        for u in range(LT):
            less = (above[k][u] == above[k][t]) & (nodes[k][u] < nodes[k][t])
            found = jnp.where(less, one, found)
        return found

    key2 = [jnp.where(above[2][t] == left, none, 2 * one) + second(2, t) for t in range(LT)]
    for t in range(LT):
        again = none
        for u in range(t):
            again = jnp.where(nodes[2][u] == nodes[2][t], one, again)
        place = again * 4 + key2[t]
        out_ref[SRC + t] = place
        out_ref[HELD + place] = jnp.int32(t)
        upper = none
        for u in range(LT):
            upper = jnp.where(nodes[2][u] == above[3][t], key2[u], upper)
        place = second(3, t) * 4 + upper
        out_ref[SRC + LT + t] = place
        out_ref[HELD + LT + place] = jnp.int32(t)
        rank = none
        for u in range(t):
            rank = rank + jnp.where(key1[u] == key1[t], one, none)
        out_ref[POS + key1[t] * 4 + rank] = jnp.int32(t)

        @pl.when(row == t)
        def _():
            out_ref[OWN] = key1[t]
            out_ref[OWN + 1] = key2[t]
            out_ref[OWN + 2] = out_ref[SRC + LT + t] % 4

    for m in (2, 3):
        for k in range(m):
            for i in range(WIDTHS[m][k]):
                q = i
                if k == 1:
                    q = out_ref[OWN] * 2 + i
                if k == 2:
                    q = out_ref[OWN + 1]
                tile = out_ref[HELD + (m - 2) * LT + core * 4 + q]
                at = KEEP + (m - 2) * 16 + k * 4 + i
                out_ref[at] = structure_ref[node_ref[m, tile], k, row]
                out_ref[at + 32] = tile


def make_table(parent, tile_node, structure, row_tile):
    ids = jnp.stack([lax.axis_index("narrow"), row_tile]).astype(jnp.int32)
    return pl.pallas_call(
        table_body,
        in_specs=[pl.BlockSpec(memory_space=pltpu.SMEM)] * 4,
        out_specs=pl.BlockSpec(memory_space=pltpu.SMEM),
        out_shape=jax.ShapeDtypeStruct((128,), jnp.int32),
    )(ids, parent, tile_node, structure)


PAIRS = ((0, 2), (1, 2), (0, 3), (1, 3), (2, 3))


def pack_body(id_ref, table_ref, own_ref, other_ref, two_ref, three_ref):
    half = LT // 2
    for b, (k, m) in enumerate(PAIRS):
        out = two_ref if m == 2 else three_ref
        base = sum(WIDTHS[m][:k])
        for i in range(WIDTHS[m][k]):
            at = KEEP + (m - 2) * 16 + k * 4 + i
            tile = table_ref[at + 32]
            keep = table_ref[at] > 0
            mine = tile // half == id_ref[0]
            start = pl.multiple_of(tile % half * TILE, TILE)
            cols = slice((base + i) * TILE, (base + i + 1) * TILE)

            @pl.when(keep & mine)
            def _():
                out[:, cols] = own_ref[b, :, pl.ds(start, TILE)]

            @pl.when(keep & jnp.logical_not(mine))
            def _():
                out[:, cols] = other_ref[b, :, pl.ds(start, TILE)]

            @pl.when(jnp.logical_not(keep))
            def _():
                out[:, cols] = jnp.zeros((out.shape[0], TILE), BF)


def packed(factor, table):
    r = factor.shape[1]
    own = jnp.stack([factor[k, :, m, :] for k, m in PAIRS])
    other = lax.ppermute(own, "narrow", [(0, 1), (1, 0)])
    whole = pl.BlockSpec(memory_space=pltpu.VMEM)
    scalar = pl.BlockSpec(memory_space=pltpu.SMEM)
    return pl.pallas_call(
        pack_body,
        in_specs=[scalar, scalar, whole, whole],
        out_specs=(whole, whole),
        out_shape=tuple(jax.ShapeDtypeStruct((r, sum(WIDTHS[m]) * TILE), BF) for m in (2, 3)),
        compiler_params=pltpu.CompilerParams(vmem_limit_bytes=VMEM),
        cost_estimate=pl.CostEstimate(flops=1, bytes_accessed=1, transcendentals=0),
    )(lax.axis_index("narrow").astype(jnp.int32).reshape(1), table, own, other)


def sparse_body(level, rows_n, mirror, table_ref, *refs):
    row_refs = [refs[q * level : (q + 1) * level] for q in range(rows_n)]
    refs = refs[rows_n * level :]
    piece_refs, out_ref, lhs = refs[:level], refs[level], refs[level + 1]
    r = row_refs[0][0].shape[0]
    span = LT * TILE
    per = TILE // r
    q = pl.program_id(0)

    @pl.when(q == 0)
    def _():
        for p in range(rows_n):
            for j in range(level):
                lhs[p * r : (p + 1) * r, j * span : (j + 1) * span] = row_refs[p][j][...]

    if mirror:
        q = table_ref[OWN + level - 1]
    total = jnp.dot(lhs[:, :span], piece_refs[0][...].reshape(span, TILE), preferred_element_type=F32)
    for j in range(1, level):
        for i in range(4 // j):
            if j == 1:
                tile = table_ref[POS + q // 2 * 4 + i]
            else:
                tile = table_ref[HELD + i * 4 + q]
            start = pl.multiple_of(j * span + tile * TILE, TILE)
            block = piece_refs[j][pl.ds(tile * per, per)].reshape(TILE, TILE)
            total += jnp.dot(lhs[:, pl.ds(start, TILE)], block, preferred_element_type=F32)
    if mirror:
        out_ref[...] = total
    else:
        for p in range(rows_n):
            value = -total[p * r : (p + 1) * r]
            if p == 1:
                value = jnp.where(table_ref[OWN] == q // 2, value, 0.0)
            if p == 2:
                value = jnp.where(table_ref[OWN + 1] == q, value, 0.0)
            out_ref[p] = value.astype(BF)


def sparse_product(level, table, rows, panel, mirror):
    wide, r, _ = panel.shape
    rows_n = len(rows)

    def column(j):
        def index(i, t):
            q = t[OWN + level - 1] if mirror else i
            if j == 0:
                return (0, 0, q)
            if j == 1:
                return (0, 0, 4 + q % 2)
            return (0, 0, 6)

        return index

    whole = pl.BlockSpec(memory_space=pltpu.VMEM)
    flat = [x for row in rows for x in row]
    specs = [whole] * len(flat) + [pl.BlockSpec((wide, r, TILE), column(j)) for j in range(level)]
    if mirror:
        shape = jax.ShapeDtypeStruct((r, TILE), F32)
        out_spec = pl.BlockSpec((r, TILE), lambda i, t: (0, 0))
    else:
        shape = jax.ShapeDtypeStruct((rows_n, r, 4 * TILE), BF)
        out_spec = pl.BlockSpec((rows_n, r, TILE), lambda i, t: (0, 0, i))
    return pl.pallas_call(
        functools.partial(sparse_body, level, rows_n, mirror),
        grid_spec=pltpu.PrefetchScalarGridSpec(
            num_scalar_prefetch=1,
            grid=(1 if mirror else 4,),
            in_specs=specs,
            out_specs=out_spec,
            scratch_shapes=[pltpu.VMEM((rows_n * r, level * LT * TILE), BF)],
        ),
        out_shape=shape,
        compiler_params=pltpu.CompilerParams(vmem_limit_bytes=VMEM),
        cost_estimate=pl.CostEstimate(flops=1, bytes_accessed=1, transcendentals=0),
    )(table, *flat, *[panel] * level)


def place_body(level, levels, id_ref, table_ref, own_ref, other_ref, slots_ref, full_ref):
    r = own_ref.shape[1]
    part = r // 2
    per = TILE // r
    me = id_ref[0]
    first = pl.multiple_of(me * part, part)
    for c in range(LT):
        source = table_ref[SRC + (level - 2) * LT + c]
        start = pl.multiple_of(source % 4 * TILE, TILE)

        def put(ref):
            for k in range(levels):
                full_ref[k, :, c * TILE : (c + 1) * TILE] = ref[k, :, pl.ds(start, TILE)]
                for i in range(per):
                    at = pl.multiple_of(start + i * r, r)
                    slots_ref[c * per + i, k] = ref[k, pl.ds(first, part), pl.ds(at, r)]

        @pl.when(source // 4 == me)
        def _():
            put(own_ref)

        @pl.when(source // 4 != me)
        def _():
            put(other_ref)


def place_slots(level, table, value):
    wide = lax.axis_size("wide")
    l, r, c = value.shape
    other = lax.ppermute(value, "narrow", [(0, 1), (1, 0)])
    whole = pl.BlockSpec(memory_space=pltpu.VMEM)
    scalar = pl.BlockSpec(memory_space=pltpu.SMEM)
    return pl.pallas_call(
        functools.partial(place_body, level, l),
        in_specs=[scalar, scalar, whole, whole],
        out_specs=(whole, whole),
        out_shape=(
            jax.ShapeDtypeStruct((wide, l, r // 2, r), BF),
            jax.ShapeDtypeStruct((l, r, 2 * c), BF),
        ),
        compiler_params=pltpu.CompilerParams(vmem_limit_bytes=VMEM),
        cost_estimate=pl.CostEstimate(flops=1, bytes_accessed=1, transcendentals=0),
    )(lax.axis_index("narrow").astype(jnp.int32).reshape(1), table, value, other)


def diag_body(level, id_ref, table_ref, own_ref, other_ref, diag_ref, out_ref, low_ref):
    me, row = id_ref[0], id_ref[1]
    half = LT // 2
    base = SRC + (level - 2) * LT
    for c in range(LT):
        source = table_ref[base + c]
        same = source % 4 == table_ref[base + row] % 4
        if level == 3:
            same = row == c
        cols = slice(c * TILE, (c + 1) * TILE)
        inner = jnp.where(source // 4 == me, own_ref[...], other_ref[...])
        value = jnp.where(same, diag_ref[:, cols] - inner, 0.0)
        low_ref[:, cols] = value.astype(BF)

        @pl.when(me == c // half)
        def _():
            out_ref[:, (c % half) * TILE : (c % half + 1) * TILE] = value


def diag_block(level, table, inner, diag, row_tile):
    r, span = diag.shape
    other = lax.ppermute(inner, "narrow", [(0, 1), (1, 0)])
    ids = jnp.stack([lax.axis_index("narrow"), row_tile]).astype(jnp.int32)
    whole = pl.BlockSpec(memory_space=pltpu.VMEM)
    scalar = pl.BlockSpec(memory_space=pltpu.SMEM)
    return pl.pallas_call(
        functools.partial(diag_body, level),
        in_specs=[scalar, scalar, whole, whole, whole],
        out_specs=(whole, whole),
        out_shape=(jax.ShapeDtypeStruct((r, span // 2), F32), jax.ShapeDtypeStruct((r, span), BF)),
        compiler_params=pltpu.CompilerParams(vmem_limit_bytes=VMEM),
        cost_estimate=pl.CostEstimate(flops=1, bytes_accessed=1, transcendentals=0),
    )(ids, table, inner, other, diag)


def upper_body(id_ref, first_ref, *refs):
    news, turns, diags, out_ref = refs[0:3], refs[3:5], refs[5:7], refs[7]
    for k in range(LEV - 1):
        for m in range(LEV):
            if m == k:
                value = first_ref[0] if k == 0 else diags[k - 1][...]
            elif m > k:
                value = news[m - 1][k].astype(F32)
            else:
                value = turns[k - 1][m].astype(F32)
            out_ref[k, :, m, :] = value


def lower_body(id_ref, turn_ref, diag_ref, held_ref, out_ref):
    for m in range(LEV - 1):
        out_ref[0, :, m, :] = turn_ref[m].astype(F32)
    out_ref[0, :, LEV - 1, :] = diag_ref[...]


def upper_rows(diag_inverse, news, turns, diags):
    r, c = diag_inverse.shape[1:]
    step = min(r, 32)
    shape = jax.ShapeDtypeStruct((LEV, r, LEV, c), F32)
    specs = [pl.BlockSpec((1, step, c), lambda i, n: (0, i, 0))]
    specs += [pl.BlockSpec((m, step, c), lambda i, n: (0, i, n[0])) for m in range(1, LEV)]
    specs += [pl.BlockSpec((k, step, c), lambda i, n: (0, i, n[0])) for k in range(1, LEV - 1)]
    specs += [pl.BlockSpec((step, c), lambda i, n: (i, 0)) for k in range(1, LEV - 1)]
    return pl.pallas_call(
        upper_body,
        grid_spec=pltpu.PrefetchScalarGridSpec(
            num_scalar_prefetch=1,
            grid=(r // step,),
            in_specs=specs,
            out_specs=pl.BlockSpec((LEV - 1, step, LEV, c), lambda i, n: (0, i, 0, 0)),
        ),
        out_shape=shape,
        compiler_params=pltpu.CompilerParams(vmem_limit_bytes=VMEM),
        cost_estimate=pl.CostEstimate(flops=0, bytes_accessed=1, transcendentals=0),
    )(lax.axis_index("narrow").astype(jnp.int32).reshape(1), diag_inverse, *news, *turns, *diags)


def lower_rows(turn, diag, held):
    r, c = diag.shape
    step = min(r, 32)
    return pl.pallas_call(
        lower_body,
        grid_spec=pltpu.PrefetchScalarGridSpec(
            num_scalar_prefetch=1,
            grid=(r // step,),
            in_specs=[
                pl.BlockSpec((LEV - 1, step, c), lambda i, n: (0, i, n[0])),
                pl.BlockSpec((step, c), lambda i, n: (i, 0)),
                pl.BlockSpec(memory_space=pl.ANY),
            ],
            out_specs=pl.BlockSpec((1, step, LEV, c), lambda i, n: (LEV - 1, i, 0, 0)),
        ),
        out_shape=jax.ShapeDtypeStruct(held.shape, F32),
        input_output_aliases={3: 0},
        compiler_params=pltpu.CompilerParams(vmem_limit_bytes=VMEM),
        cost_estimate=pl.CostEstimate(flops=0, bytes_accessed=1, transcendentals=0),
    )(lax.axis_index("narrow").astype(jnp.int32).reshape(1), turn, diag, held)


def local(factor, diag_inverse, parent, tile_node, structure):
    row_count = factor.shape[1]
    col_count = factor.shape[3]
    col_tiles = col_count // TILE
    row_id = lax.axis_index("wide")
    col_id = lax.axis_index("narrow")
    high = lax.Precision.HIGHEST
    reach = ancestors(parent)
    node_hot = (tile_node[:, :, None] == jnp.arange(M, dtype=jnp.int32)[None, None, :]).astype(
        jnp.float32
    )
    row_pos = row_id * row_count // TILE
    pos_hot = (jnp.arange(LT, dtype=jnp.int32) == row_pos).astype(jnp.float32)
    row_hot = jnp.einsum("t,ltm->lm", pos_hot, node_hot, precision=high)
    col_sel = (
        jnp.arange(LT, dtype=jnp.int32)[None, :]
        == (col_id * col_tiles + jnp.arange(col_tiles, dtype=jnp.int32))[:, None]
    ).astype(jnp.float32)
    col_hot = jnp.einsum("jt,ltm->ljm", col_sel, node_hot, precision=high)
    tile_above = jnp.einsum("ra,ba,cjb->rcj", row_hot, reach, col_hot, precision=high)
    tile_same = jnp.einsum("lm,ljm->lj", row_hot, col_hot, precision=high)
    struct_row = jnp.einsum("mlt,t->ml", structure.astype(jnp.float32), pos_hot, precision=high)
    tile_struct = jnp.einsum("cjm,mr->rcj", col_hot, struct_row, precision=high)
    above = (tile_above > 0.5).astype(jnp.int32)
    same = (tile_same > 0.5).astype(jnp.int32)

    def masked(k, m):
        return (factor[k, :, m, :] * spread(tile_struct[k, m])[None, :].astype(BF))[None]

    place = positions(False)

    def panel_of(level):
        return jnp.concatenate([masked(k, level) for k in range(level)], axis=0)

    wide = lax.axis_size("wide")
    whole_place = jnp.arange(wide, dtype=jnp.int32)
    compact = lax.axis_size("narrow") == 2 and row_count % 128 == 0 and TILE % row_count == 0
    first = along_z(panel_of(1), None)
    if compact:
        table = make_table(parent, tile_node, structure, row_pos)
        shards = packed(factor, table)
        panels = {m: lax.all_gather(shards[m - 2], "wide", axis=0) for m in (2, 3)}
        wide_diag = {m: narrow_all(diag_inverse[m], 1) for m in (2, 3)}
    else:
        panels = {m: lax.all_gather(panel_of(m), "wide", axis=0) for m in (2, 3)}
    one = along_both(along_xy(first, None), None)

    rows = {0: [narrow_all(diag_inverse[0].astype(BF), 1)]}
    news, turns, diags = [], [], []
    for level in range(1, LEV):
        known = [rows[k] for k in range(level)]
        packed_here = compact and level > 1
        if packed_here:
            value = sparse_product(level, table, known, panels[level], False)
            slots, full = place_slots(level, table, value)
        else:
            if level == 1:
                groups = [((0,), place, one)]
            else:
                groups = [(tuple(range(level)), whole_place, [panels[level]])]
            value = product(known, groups, above[:level, level])
            slots, full = make_slots(value)
        news.append(full)
        for k in range(level):
            rows[k].append(full[k])
        if level == LEV - 1:
            out = upper_rows(diag_inverse, news, turns, diags)
        got = lax.all_to_all(slots, "wide", split_axis=0, concat_axis=0, tiled=True)
        turn = mirrored(got, full)
        turns.append(turn)
        rows[level] = [turn[k] for k in range(level)]
        if packed_here:
            inner = sparse_product(level, table, [rows[level]], panels[level], True)
            done, whole_low = diag_block(level, table, inner, wide_diag[level], row_pos)
        else:
            done, low = product([rows[level]], groups, same[level : level + 1], (diag_inverse, level))
            whole_low = narrow_all(low, 1) if level < LEV - 1 else None
        diags.append(done)
        if level < LEV - 1:
            rows[level].append(whole_low)
    return lower_rows(turns[-1], diags[-1], out)


def solution(mesh):
    return jax.shard_map(
        local,
        mesh=mesh,
        in_specs=(P(None, "wide", None, "narrow"), P(None, "wide", "narrow"), P(), P(), P()),
        out_specs=P(None, "wide", None, "narrow"),
        check_vma=False,
    )
```

```python
import functools

import jax
import jax.numpy as jnp
from jax import lax
from jax.experimental import pallas as pl
from jax.experimental.pallas import tpu as pltpu
from jax.sharding import PartitionSpec as P

LEV = 4
TILE = 256
LT = 8
M = 15
BF = jnp.bfloat16
F32 = jnp.float32
VMEM = 56 * 1024 * 1024


def ancestors(parent):
    node_ids = jnp.arange(M, dtype=jnp.int32)
    step_mat = (parent[:, None] == node_ids[None, :]).astype(jnp.float32)
    power_mat = step_mat
    reach = step_mat
    for hop_count in range(LEV - 2):
        power_mat = jnp.dot(power_mat, step_mat, precision=lax.Precision.HIGHEST)
        reach = reach + power_mat
    return reach


def spread(mask_tile):
    return jnp.repeat(mask_tile, TILE, axis=-1)


def after(value, *others):
    return lax.optimization_barrier((value,) + others)[0]


def narrow_all(x, axis):
    size = lax.axis_size("narrow")
    mine = lax.axis_index("narrow")
    if size == 2:
        other = lax.ppermute(x, "narrow", [(0, 1), (1, 0)])
        first = mine == 0
        return jnp.concatenate([jnp.where(first, x, other), jnp.where(first, other, x)], axis=axis)
    shape = list(x.shape)
    width = shape[axis]
    shape[axis] = width * size
    out = jnp.zeros(shape, x.dtype)
    for hop in range(size):
        got = x if hop == 0 else lax.ppermute(x, "narrow", [(i, (i + hop) % size) for i in range(size)])
        out = lax.dynamic_update_slice_in_dim(out, got, (mine - hop) % size * width, axis)
    return out


def swap(value, turn):
    wide = lax.axis_size("wide")
    narrow = lax.axis_size("narrow")
    pairs = []
    for i in range(wide):
        for j in range(narrow):
            pairs.append((i * narrow + j, (i ^ (1 if (j + turn) % 2 == 0 else 2)) * narrow + j))
    return lax.ppermute(value, ("wide", "narrow"), pairs)


def shifts(value):
    wide = lax.axis_size("wide")
    return [value] + [
        lax.ppermute(value, "wide", [(i, (i + 4 * hop) % wide) for i in range(wide)])
        for hop in range(1, wide // 4)
    ]


def positions(z_last):
    wide = lax.axis_size("wide")
    depth = wide // 4
    row_id = lax.axis_index("wide")
    odd = lax.axis_index("narrow") % 2
    z = (row_id // 4 - jnp.arange(depth, dtype=jnp.int32)) % depth
    flips = jnp.stack([0 * odd, 1 + odd, 2 - odd, 3 + 0 * odd])
    near = (row_id % 4) ^ flips
    if z_last:
        return (z[:, None] * 4 + near[None, :]).reshape(-1).astype(jnp.int32)
    return (z[None, :] * 4 + near[:, None]).reshape(-1).astype(jnp.int32)


def along_z(x, gate):
    return shifts(x if gate is None else after(x, gate))


def along_xy(pieces, gate):
    if gate is not None:
        held = lax.optimization_barrier(tuple(pieces) + (gate,))
        pieces = held[:-1]
    line = jnp.stack(pieces)
    return [line, swap(line, 0), swap(line, 1)]


def along_both(arrays, gate):
    near = arrays[1]
    return arrays + [swap(near if gate is None else after(near, *gate), 1)]


def product_body(plan, rows_n, steps_n, finish, *refs):
    place_ref, mask_ref = refs[0], refs[1]
    refs = refs[2:]
    row_refs = [refs[q * steps_n : (q + 1) * steps_n] for q in range(rows_n)]
    refs = refs[rows_n * steps_n :]
    count = sum(arrays for _, arrays, _ in plan)
    piece_refs, refs = refs[:count], refs[count:]
    if finish:
        diag_ref, out_ref, low_ref, lhs = refs
    else:
        out_ref, lhs = refs
    r = row_refs[0][0].shape[0]
    width = piece_refs[0].shape[-1]

    @pl.when(pl.program_id(0) == 0)
    def _():
        at = 0
        for g, (levels, arrays, each) in enumerate(plan):
            for i in range(arrays * each):
                start = pl.multiple_of(place_ref[g, i] * r, r)
                for j in levels:
                    for q in range(rows_n):
                        lhs[q * r : (q + 1) * r, at : at + r] = row_refs[q][j][:, pl.ds(start, r)]
                    at += r

    total = None
    at, base = 0, 0
    for levels, arrays, each in plan:
        depth = each * len(levels) * r
        for a in range(arrays):
            part = jnp.dot(
                lhs[:, at : at + depth],
                piece_refs[base + a][...].reshape(depth, width),
                preferred_element_type=F32,
            )
            total = part if total is None else total + part
            at += depth
        base += arrays
    here = pl.program_id(0)
    for q in range(rows_n):
        for t in range(width // TILE):
            keep = mask_ref[q, here * (width // TILE) + t] > 0
            cols = slice(t * TILE, (t + 1) * TILE)
            value = total[q * r : (q + 1) * r, cols]
            if finish:
                value = diag_ref[0, :, cols] - value
            else:
                value = -value
            value = jnp.where(keep, value, 0.0)
            if finish:
                out_ref[:, cols] = value
                low_ref[:, cols] = value.astype(BF)
            else:
                out_ref[q, :, cols] = value.astype(BF)


def product(rows, groups, mask, diag=None, shift=0):
    r = rows[0][0].shape[0]
    c = groups[0][2][0].shape[-1]
    rows_n, steps_n = len(rows), len(rows[0])
    if r % 128:
        total = 0.0
        for levels, place, arrays in groups:
            at = 0
            for array in arrays:
                each = array.shape[0]
                here = place[at : at + each]
                lhs = jnp.concatenate(
                    [
                        jnp.stack(
                            [jnp.take(row[j].reshape(r, -1, r), here, axis=1) for j in levels], axis=2
                        ).reshape(r, -1)
                        for row in rows
                    ],
                    axis=0,
                )
                total += jnp.dot(lhs, array.reshape(-1, c), preferred_element_type=F32)
                at += each
        total = total.reshape(rows_n, r, c)
        keep = jnp.repeat(mask, TILE, axis=1)[:, None, :] > 0
        if diag is None:
            return jnp.where(keep, -total, 0.0).astype(BF)
        level = diag[1]
        value = jnp.where(keep[0], diag[0][level, :, shift : shift + c] - total[0], 0.0)
        return value, value.astype(BF)
    width = TILE
    plan = tuple((tuple(levels), len(arrays), arrays[0].shape[0]) for levels, _, arrays in groups)
    place = jnp.stack([p for _, p, _ in groups])
    whole = pl.BlockSpec(memory_space=pltpu.VMEM)
    scalar = pl.BlockSpec(memory_space=pltpu.SMEM)
    pieces = [a for _, _, arrays in groups for a in arrays]
    piece_specs = [pl.BlockSpec(a.shape[:3] + (width,), lambda i: (0, 0, 0, i)) for a in pieces]
    flat = [x for row in rows for x in row]
    operands = [place, mask] + flat + pieces
    specs = [scalar, scalar] + [whole] * len(flat) + piece_specs
    if diag is None:
        outs = jax.ShapeDtypeStruct((rows_n, r, c), BF)
        out_specs = pl.BlockSpec((rows_n, r, width), lambda i: (0, 0, i))
    else:
        level = diag[1]
        skip = shift // width
        operands.append(diag[0])
        specs.append(pl.BlockSpec((1, r, width), lambda i: (level, 0, skip + i)))
        outs = (jax.ShapeDtypeStruct((r, c), F32), jax.ShapeDtypeStruct((r, c), BF))
        out_specs = (pl.BlockSpec((r, width), lambda i: (0, i)),) * 2
    deep = sum(len(levels) * arrays * each for levels, arrays, each in plan) * r
    return pl.pallas_call(
        functools.partial(product_body, plan, rows_n, steps_n, diag is not None),
        grid=(c // width,),
        in_specs=specs,
        out_specs=out_specs,
        out_shape=outs,
        scratch_shapes=[pltpu.VMEM((rows_n * r, deep), BF)],
        compiler_params=pltpu.CompilerParams(vmem_limit_bytes=VMEM),
        cost_estimate=pl.CostEstimate(
            flops=1, bytes_accessed=1, transcendentals=0
        ),
    )(*operands)


def slots_body(levels, wide, id_ref, own_ref, other_ref, slots_ref, full_ref):
    r, c = own_ref.shape[1:]
    part = r // 2
    half = wide // 2
    for n in range(2):

        @pl.when(id_ref[0] == n)
        def _():
            for h in range(2):
                ref = own_ref if h == n else other_ref
                for k in range(levels):
                    full_ref[k, :, h * c : (h + 1) * c] = ref[k]
                    for i in range(half):
                        slots_ref[h * half + i, k] = ref[k, n * part : (n + 1) * part, i * r : (i + 1) * r]


def make_slots(value):
    wide = lax.axis_size("wide")
    narrow = lax.axis_size("narrow")
    l, r, c = value.shape
    if narrow != 2 or r % 128:
        full = narrow_all(value, 2)
        part = r // narrow
        mine = lax.dynamic_slice_in_dim(full, lax.axis_index("narrow") * part, part, 1)
        return mine.reshape(l, part, wide, r).transpose(2, 0, 1, 3), full
    other = lax.ppermute(value, "narrow", [(0, 1), (1, 0)])
    whole = pl.BlockSpec(memory_space=pltpu.VMEM)
    return pl.pallas_call(
        functools.partial(slots_body, l, wide),
        in_specs=[pl.BlockSpec(memory_space=pltpu.SMEM), whole, whole],
        out_specs=(whole, whole),
        out_shape=(
            jax.ShapeDtypeStruct((wide, l, r // 2, r), BF),
            jax.ShapeDtypeStruct((l, r, 2 * c), BF),
        ),
        compiler_params=pltpu.CompilerParams(vmem_limit_bytes=VMEM),
        cost_estimate=pl.CostEstimate(flops=1, bytes_accessed=1, transcendentals=0),
    )(lax.axis_index("narrow").astype(jnp.int32).reshape(1), value, other)


def turn_body(levels, wide, id_ref, own_ref, other_ref, out_ref):
    r = out_ref.shape[1]
    for n in range(2):

        @pl.when(id_ref[0] == n)
        def _():
            first, second = (own_ref, other_ref) if n == 0 else (other_ref, own_ref)
            for k in range(levels):
                for w in range(wide):
                    block = jnp.concatenate([first[w, k], second[w, k]], axis=0)
                    out_ref[k, :, w * r : (w + 1) * r] = block.T


def mirrored(got, full):
    wide = lax.axis_size("wide")
    narrow = lax.axis_size("narrow")
    l, r, cols = full.shape
    if narrow != 2 or r % 128:
        return narrow_all(got, 2).transpose(1, 3, 0, 2).reshape(l, r, cols)
    other = lax.ppermute(got, "narrow", [(0, 1), (1, 0)])
    whole = pl.BlockSpec(memory_space=pltpu.VMEM)
    return pl.pallas_call(
        functools.partial(turn_body, l, wide),
        in_specs=[pl.BlockSpec(memory_space=pltpu.SMEM), whole, whole],
        out_specs=whole,
        out_shape=jax.ShapeDtypeStruct((l, r, cols), BF),
        compiler_params=pltpu.CompilerParams(vmem_limit_bytes=VMEM),
        cost_estimate=pl.CostEstimate(flops=1, bytes_accessed=1, transcendentals=0),
    )(lax.axis_index("narrow").astype(jnp.int32).reshape(1), got, other)


SRC, POS, HELD, OWN, KEEP = 0, 16, 24, 40, 48
WIDTHS = {2: (4, 2), 3: (4, 2, 1)}


def table_body(id_ref, parent_ref, node_ref, structure_ref, out_ref):
    core, row = id_ref[0], id_ref[1]
    for i in range(out_ref.shape[0]):
        out_ref[i] = jnp.int32(0)
    one, none = jnp.int32(1), jnp.int32(0)
    nodes = [[node_ref[k, t] for t in range(LT)] for k in range(LEV)]
    above = [[parent_ref[nodes[k][t]] for t in range(LT)] for k in range(LEV)]
    left = nodes[1][0]
    key1 = [jnp.where(nodes[1][t] == left, none, one) for t in range(LT)]

    def second(k, t):
        found = none
        for u in range(LT):
            less = (above[k][u] == above[k][t]) & (nodes[k][u] < nodes[k][t])
            found = jnp.where(less, one, found)
        return found

    key2 = [jnp.where(above[2][t] == left, none, 2 * one) + second(2, t) for t in range(LT)]
    for t in range(LT):
        again = none
        for u in range(t):
            again = jnp.where(nodes[2][u] == nodes[2][t], one, again)
        place = again * 4 + key2[t]
        out_ref[SRC + t] = place
        out_ref[HELD + place] = jnp.int32(t)
        upper = none
        for u in range(LT):
            upper = jnp.where(nodes[2][u] == above[3][t], key2[u], upper)
        place = second(3, t) * 4 + upper
        out_ref[SRC + LT + t] = place
        out_ref[HELD + LT + place] = jnp.int32(t)
        rank = none
        for u in range(t):
            rank = rank + jnp.where(key1[u] == key1[t], one, none)
        out_ref[POS + key1[t] * 4 + rank] = jnp.int32(t)

        @pl.when(row == t)
        def _():
            out_ref[OWN] = key1[t]
            out_ref[OWN + 1] = key2[t]
            out_ref[OWN + 2] = out_ref[SRC + LT + t] % 4

    for m in (2, 3):
        for k in range(m):
            for i in range(WIDTHS[m][k]):
                q = i
                if k == 1:
                    q = out_ref[OWN] * 2 + i
                if k == 2:
                    q = out_ref[OWN + 1]
                tile = out_ref[HELD + (m - 2) * LT + core * 4 + q]
                at = KEEP + (m - 2) * 16 + k * 4 + i
                out_ref[at] = structure_ref[node_ref[m, tile], k, row]
                out_ref[at + 32] = tile


def make_table(parent, tile_node, structure, row_tile):
    ids = jnp.stack([lax.axis_index("narrow"), row_tile]).astype(jnp.int32)
    return pl.pallas_call(
        table_body,
        in_specs=[pl.BlockSpec(memory_space=pltpu.SMEM)] * 4,
        out_specs=pl.BlockSpec(memory_space=pltpu.SMEM),
        out_shape=jax.ShapeDtypeStruct((128,), jnp.int32),
    )(ids, parent, tile_node, structure)


PAIRS = ((0, 2), (1, 2), (0, 3), (1, 3), (2, 3))


def pack_body(id_ref, table_ref, own_ref, other_ref, two_ref, three_ref):
    half = LT // 2
    for b, (k, m) in enumerate(PAIRS):
        out = two_ref if m == 2 else three_ref
        base = sum(WIDTHS[m][:k])
        for i in range(WIDTHS[m][k]):
            at = KEEP + (m - 2) * 16 + k * 4 + i
            tile = table_ref[at + 32]
            keep = table_ref[at] > 0
            mine = tile // half == id_ref[0]
            start = pl.multiple_of(tile % half * TILE, TILE)
            cols = slice((base + i) * TILE, (base + i + 1) * TILE)

            @pl.when(keep & mine)
            def _():
                out[:, cols] = own_ref[b, :, pl.ds(start, TILE)]

            @pl.when(keep & jnp.logical_not(mine))
            def _():
                out[:, cols] = other_ref[b, :, pl.ds(start, TILE)]

            @pl.when(jnp.logical_not(keep))
            def _():
                out[:, cols] = jnp.zeros((out.shape[0], TILE), BF)


def packed(factor, table):
    r = factor.shape[1]
    own = jnp.stack([factor[k, :, m, :] for k, m in PAIRS])
    other = lax.ppermute(own, "narrow", [(0, 1), (1, 0)])
    whole = pl.BlockSpec(memory_space=pltpu.VMEM)
    scalar = pl.BlockSpec(memory_space=pltpu.SMEM)
    return pl.pallas_call(
        pack_body,
        in_specs=[scalar, scalar, whole, whole],
        out_specs=(whole,) * 2,
        out_shape=tuple(jax.ShapeDtypeStruct((r, sum(WIDTHS[m]) * TILE), BF) for m in (2, 3)),
        compiler_params=pltpu.CompilerParams(vmem_limit_bytes=VMEM),
        cost_estimate=pl.CostEstimate(flops=1, bytes_accessed=1, transcendentals=0),
    )(lax.axis_index("narrow").astype(jnp.int32).reshape(1), table, own, other)


def sparse_body(level, shapes, mirror, table_ref, place_ref, *refs):
    row_refs, refs = refs[: len(shapes)], refs[len(shapes) :]
    out_ref, lhs, rest = refs[-3:]
    piece_refs = refs[:-3]
    r = row_refs[0].shape[-2]
    span = LT * TILE
    per = TILE // r
    q = pl.program_id(0)

    @pl.when(q == 0)
    def _():
        for ref, (_, many, at) in zip(row_refs, shapes, strict=True):
            for p in range(many):
                row, j = at[p]
                block = ref[p] if len(ref.shape) == 3 else ref[...]
                lhs[row * r : (row + 1) * r, j * span : (j + 1) * span] = block
        if level == 3:
            each = piece_refs[0].shape[0]
            for a in range(4):
                for i in range(each):
                    rest[place_ref[a * each + i]] = piece_refs[a][i]

    if mirror:
        q = table_ref[OWN + level - 1]
    if level == 3:
        block = rest[:, :, pl.ds(pl.multiple_of(q * TILE, TILE), TILE)]
    else:
        block = piece_refs[0][...]
    total = jnp.dot(lhs[:, :span], block.reshape(span, TILE), preferred_element_type=F32)
    for j in range(1, level):
        for i in range(4 // j):
            if j == 1:
                tile = table_ref[POS + q // 2 * 4 + i]
            else:
                tile = table_ref[HELD + i * 4 + q]
            start = pl.multiple_of(j * span + tile * TILE, TILE)
            if level == 2:
                block = piece_refs[1][pl.ds(tile * per, per)]
            elif j == 1:
                block = rest[pl.ds(tile * per, per), :, pl.ds(pl.multiple_of((4 + q % 2) * TILE, TILE), TILE)]
            else:
                block = rest[pl.ds(tile * per, per), :, 6 * TILE : 7 * TILE]
            total += jnp.dot(
                lhs[:, pl.ds(start, TILE)], block.reshape(TILE, TILE), preferred_element_type=F32
            )
    if mirror:
        out_ref[...] = total
    else:
        for p in range(level):
            value = -total[p * r : (p + 1) * r]
            if p == 1:
                value = jnp.where(table_ref[OWN] == q // 2, value, 0.0)
            if p == 2:
                value = jnp.where(table_ref[OWN + 1] == q, value, 0.0)
            out_ref[p] = value.astype(BF)


def sparse_product(level, table, place, rows, panel, rest, mirror):
    wide = lax.axis_size("wide")
    r = rows[0][0].shape[-2]
    rows_n = 1 if mirror else level

    def column(j):
        def index(i, t):
            q = t[OWN + level - 1] if mirror else i
            return (0, 0, q if j == 0 else 4 + q % 2)

        return index

    whole = pl.BlockSpec(memory_space=pltpu.VMEM)
    flat = [array for array, _ in rows]
    shapes = tuple((0, len(at), at) for _, at in rows)
    specs = [pl.BlockSpec(memory_space=pltpu.SMEM)] + [whole] * len(flat)
    operands = [table, place] + flat
    for j in range(0 if level == 3 else 2):
        specs.append(pl.BlockSpec((wide, r, TILE), column(j)))
        operands.append(panel)
    specs += [whole] * len(rest)
    operands += rest
    if mirror:
        shape = jax.ShapeDtypeStruct((r, TILE), F32)
        out_spec = pl.BlockSpec((r, TILE), lambda i, t: (0, 0))
    else:
        shape = jax.ShapeDtypeStruct((rows_n, r, 4 * TILE), BF)
        out_spec = pl.BlockSpec((rows_n, r, TILE), lambda i, t: (0, 0, i))
    spare = (wide, r, 7 * TILE) if level == 3 else (1, 16, 128)
    return pl.pallas_call(
        functools.partial(sparse_body, level, shapes, mirror),
        grid_spec=pltpu.PrefetchScalarGridSpec(
            num_scalar_prefetch=1,
            grid=(1 if mirror else 4,),
            in_specs=specs,
            out_specs=out_spec,
            scratch_shapes=[
                pltpu.VMEM((rows_n * r, level * LT * TILE), BF),
                pltpu.VMEM(spare, BF),
            ],
        ),
        out_shape=shape,
        compiler_params=pltpu.CompilerParams(vmem_limit_bytes=VMEM),
        cost_estimate=pl.CostEstimate(flops=1, bytes_accessed=1, transcendentals=0),
    )(*operands)


def place_body(level, levels, id_ref, table_ref, own_ref, other_ref, slots_ref, full_ref):
    r = own_ref.shape[1]
    part = r // 2
    per = TILE // r
    me = id_ref[0]
    first = pl.multiple_of(me * part, part)
    for c in range(LT):
        source = table_ref[SRC + (level - 2) * LT + c]
        start = pl.multiple_of(source % 4 * TILE, TILE)

        def put(ref):
            for k in range(levels):
                full_ref[k, :, c * TILE : (c + 1) * TILE] = ref[k, :, pl.ds(start, TILE)]
                for i in range(per):
                    at = pl.multiple_of(start + i * r, r)
                    slots_ref[c * per + i, k] = ref[k, pl.ds(first, part), pl.ds(at, r)]

        @pl.when(source // 4 == me)
        def _():
            put(own_ref)

        @pl.when(source // 4 != me)
        def _():
            put(other_ref)


def place_slots(level, table, value):
    wide = lax.axis_size("wide")
    l, r, c = value.shape
    other = lax.ppermute(value, "narrow", [(0, 1), (1, 0)])
    whole = pl.BlockSpec(memory_space=pltpu.VMEM)
    scalar = pl.BlockSpec(memory_space=pltpu.SMEM)
    return pl.pallas_call(
        functools.partial(place_body, level, l),
        in_specs=[scalar, scalar, whole, whole],
        out_specs=(whole, whole),
        out_shape=(
            jax.ShapeDtypeStruct((wide, l, r // 2, r), BF),
            jax.ShapeDtypeStruct((l, r, 2 * c), BF),
        ),
        compiler_params=pltpu.CompilerParams(vmem_limit_bytes=VMEM),
        cost_estimate=pl.CostEstimate(flops=1, bytes_accessed=1, transcendentals=0),
    )(lax.axis_index("narrow").astype(jnp.int32).reshape(1), table, value, other)


def diag_body(level, id_ref, table_ref, own_ref, other_ref, diag_ref, out_ref, low_ref):
    me, row = id_ref[0], id_ref[1]
    half = LT // 2
    base = SRC + (level - 2) * LT
    for c in range(LT):
        source = table_ref[base + c]
        same = source % 4 == table_ref[base + row] % 4
        if level == 3:
            same = row == c
        cols = slice(c * TILE, (c + 1) * TILE)
        inner = jnp.where(source // 4 == me, own_ref[...], other_ref[...])
        value = jnp.where(same, diag_ref[:, cols] - inner, 0.0)
        low_ref[:, cols] = value.astype(BF)

        @pl.when(me == c // half)
        def _():
            out_ref[:, (c % half) * TILE : (c % half + 1) * TILE] = value


def diag_block(level, table, inner, diag, row_tile):
    r, span = diag.shape
    other = lax.ppermute(inner, "narrow", [(0, 1), (1, 0)])
    ids = jnp.stack([lax.axis_index("narrow"), row_tile]).astype(jnp.int32)
    whole = pl.BlockSpec(memory_space=pltpu.VMEM)
    scalar = pl.BlockSpec(memory_space=pltpu.SMEM)
    return pl.pallas_call(
        functools.partial(diag_body, level),
        in_specs=[scalar, scalar, whole, whole, whole],
        out_specs=(whole, whole),
        out_shape=(jax.ShapeDtypeStruct((r, span // 2), F32), jax.ShapeDtypeStruct((r, span), BF)),
        compiler_params=pltpu.CompilerParams(vmem_limit_bytes=VMEM),
        cost_estimate=pl.CostEstimate(flops=1, bytes_accessed=1, transcendentals=0),
    )(ids, table, inner, other, diag)


def upper_body(id_ref, first_ref, *refs):
    news, turns, diags, out_ref = refs[0:3], refs[3:5], refs[5:7], refs[7]
    for k in range(LEV - 1):
        for m in range(LEV):
            if m == k:
                value = first_ref[0] if k == 0 else diags[k - 1][...]
            elif m > k:
                value = news[m - 1][k].astype(F32)
            else:
                value = turns[k - 1][m].astype(F32)
            out_ref[k, :, m, :] = value


def lower_body(id_ref, turn_ref, diag_ref, held_ref, out_ref):
    for m in range(LEV - 1):
        out_ref[0, :, m, :] = turn_ref[m].astype(F32)
    out_ref[0, :, LEV - 1, :] = diag_ref[...]


def upper_rows(diag_inverse, news, turns, diags):
    r, c = diag_inverse.shape[1:]
    step = min(r, 32)
    shape = jax.ShapeDtypeStruct((LEV, r, LEV, c), F32)
    specs = [pl.BlockSpec((1, step, c), lambda i, n: (0, i, 0))]
    specs += [pl.BlockSpec((m, step, c), lambda i, n: (0, i, n[0])) for m in range(1, LEV)]
    specs += [pl.BlockSpec((k, step, c), lambda i, n: (0, i, n[0])) for k in range(1, LEV - 1)]
    specs += [pl.BlockSpec((step, c), lambda i, n: (i, 0)) for k in range(1, LEV - 1)]
    return pl.pallas_call(
        upper_body,
        grid_spec=pltpu.PrefetchScalarGridSpec(
            num_scalar_prefetch=1,
            grid=(r // step,),
            in_specs=specs,
            out_specs=pl.BlockSpec((LEV - 1, step, LEV, c), lambda i, n: (0, i, 0, 0)),
        ),
        out_shape=shape,
        compiler_params=pltpu.CompilerParams(vmem_limit_bytes=VMEM),
        cost_estimate=pl.CostEstimate(flops=0, bytes_accessed=40 * 2**20, transcendentals=0),
    )(lax.axis_index("narrow").astype(jnp.int32).reshape(1), diag_inverse, *news, *turns, *diags)


def lower_rows(turn, diag, held):
    r, c = diag.shape
    step = min(r, 32)
    return pl.pallas_call(
        lower_body,
        grid_spec=pltpu.PrefetchScalarGridSpec(
            num_scalar_prefetch=1,
            grid=(r // step,),
            in_specs=[
                pl.BlockSpec((LEV - 1, step, c), lambda i, n: (0, i, n[0])),
                pl.BlockSpec((step, c), lambda i, n: (i, 0)),
                pl.BlockSpec(memory_space=pl.ANY),
            ],
            out_specs=pl.BlockSpec((1, step, LEV, c), lambda i, n: (LEV - 1, i, 0, 0)),
        ),
        out_shape=jax.ShapeDtypeStruct(held.shape, F32),
        input_output_aliases={3: 0},
        compiler_params=pltpu.CompilerParams(vmem_limit_bytes=VMEM),
        cost_estimate=pl.CostEstimate(flops=0, bytes_accessed=1, transcendentals=0),
    )(lax.axis_index("narrow").astype(jnp.int32).reshape(1), turn, diag, held)


def local(factor, diag_inverse, parent, tile_node, structure):
    row_count = factor.shape[1]
    col_count = factor.shape[3]
    col_tiles = col_count // TILE
    row_id = lax.axis_index("wide")
    col_id = lax.axis_index("narrow")
    high = lax.Precision.HIGHEST
    reach = ancestors(parent)
    node_hot = (tile_node[:, :, None] == jnp.arange(M, dtype=jnp.int32)[None, None, :]).astype(
        jnp.float32
    )
    row_pos = row_id * row_count // TILE
    pos_hot = (jnp.arange(LT, dtype=jnp.int32) == row_pos).astype(jnp.float32)
    row_hot = jnp.einsum("t,ltm->lm", pos_hot, node_hot, precision=high)
    col_sel = (
        jnp.arange(LT, dtype=jnp.int32)[None, :]
        == (col_id * col_tiles + jnp.arange(col_tiles, dtype=jnp.int32))[:, None]
    ).astype(jnp.float32)
    col_hot = jnp.einsum("jt,ltm->ljm", col_sel, node_hot, precision=high)
    tile_above = jnp.einsum("ra,ba,cjb->rcj", row_hot, reach, col_hot, precision=high)
    tile_same = jnp.einsum("lm,ljm->lj", row_hot, col_hot, precision=high)
    struct_row = jnp.einsum("mlt,t->ml", structure.astype(jnp.float32), pos_hot, precision=high)
    tile_struct = jnp.einsum("cjm,mr->rcj", col_hot, struct_row, precision=high)
    above = (tile_above > 0.5).astype(jnp.int32)
    same = (tile_same > 0.5).astype(jnp.int32)

    def masked(k, m):
        return (factor[k, :, m, :] * spread(tile_struct[k, m])[None, :].astype(BF))[None]

    place = positions(False)

    def panel_of(level):
        return jnp.concatenate([masked(k, level) for k in range(level)], axis=0)

    wide = lax.axis_size("wide")
    whole_place = jnp.arange(wide, dtype=jnp.int32)
    compact = lax.axis_size("narrow") == 2 and row_count % 128 == 0 and TILE % row_count == 0
    first = along_z(panel_of(1), None)
    if compact:
        table = make_table(parent, tile_node, structure, row_pos)
        shards = packed(factor, table)
        panels = {2: lax.all_gather(shards[0], "wide", axis=0), 3: None}
        wide_diag = {m: narrow_all(diag_inverse[m], 1) for m in (2, 3)}
    else:
        panels = {m: lax.all_gather(panel_of(m), "wide", axis=0) for m in (2, 3)}
    one = along_xy(first, None)
    if compact:
        third = along_z(after(shards[1], one[0]), None)
    one = along_both(one, (one[2],) + tuple(third) if compact else None)

    held = {}
    rows = {0: [(narrow_all(diag_inverse[0].astype(BF), 1), ((0, 0),))]}
    news, turns, diags = [], [], []
    rest = []
    for level in range(1, LEV):
        packed_here = compact and level > 1
        if packed_here:
            known = [part for k in range(level) for part in rows[k]] + [held[m] for m in range(1, level)]
            if level == 2:
                rest = along_xy(third, panels[2])
            value = sparse_product(level, table, place, known, panels[level], rest if level == 3 else [], False)
            slots, full = place_slots(level, table, value)
        else:
            if level == 1:
                groups = [((0,), place, one)]
                known = [[rows[0][0][0]]]
            else:
                groups = [(tuple(range(level)), whole_place, [panels[level]])]
                known = []
                for k in range(level):
                    by_level = {}
                    for array, at in rows[k] + [held[m] for m in range(1, level)]:
                        for p, (row, j) in enumerate(at):
                            if row == k:
                                by_level[j] = array[p] if array.ndim == 3 else array
                    known.append([by_level[j] for j in range(level)])
            value = product(known, groups, above[:level, level])
            slots, full = make_slots(value)
        news.append(full)
        held[level] = (full, tuple((k, level) for k in range(level)))
        if level == LEV - 1:
            out = upper_rows(diag_inverse, news, turns, diags)
        got = lax.all_to_all(slots, "wide", split_axis=0, concat_axis=0, tiled=True)
        if packed_here and level == 2:
            rest = along_both(rest, (slots,))
            got = after(got, rest[1], rest[2])
        turn = mirrored(got, full)
        turns.append(turn)
        rows[level] = [(turn, tuple((level, j) for j in range(level)))]
        if packed_here:
            here = [(turn, tuple((0, j) for j in range(level)))]
            inner = sparse_product(level, table, place, here, panels[level], rest if level == 3 else [], True)
            done, whole_low = diag_block(level, table, inner, wide_diag[level], row_pos)
        else:
            known = [[turn[k] for k in range(level)]]
            done, low = product(known, groups, same[level : level + 1], (diag_inverse, level))
            whole_low = narrow_all(low, 1) if level < LEV - 1 else None
        diags.append(done)
        if level < LEV - 1:
            rows[level].append((whole_low, ((level, level),)))
    return lower_rows(turns[-1], diags[-1], out)


def solution(mesh):
    return jax.shard_map(
        local,
        mesh=mesh,
        in_specs=(P(None, "wide", None, "narrow"), P(None, "wide", "narrow"), P(), P(), P()),
        out_specs=P(None, "wide", None, "narrow"),
        check_vma=False,
    )
```

```python
import functools

import jax
import jax.numpy as jnp
from jax import lax
from jax.experimental import pallas as pl
from jax.experimental.pallas import tpu as pltpu
from jax.sharding import PartitionSpec as P

LEV = 4
TILE = 256
LT = 8
M = 15
BF = jnp.bfloat16
F32 = jnp.float32
VMEM = 56 * 1024 * 1024


def ancestors(parent):
    node_ids = jnp.arange(M, dtype=jnp.int32)
    step_mat = (parent[:, None] == node_ids[None, :]).astype(jnp.float32)
    power_mat = step_mat
    reach = step_mat
    for hop_count in range(LEV - 2):
        power_mat = jnp.dot(power_mat, step_mat, precision=lax.Precision.HIGHEST)
        reach = reach + power_mat
    return reach


def spread(mask_tile):
    return jnp.repeat(mask_tile, TILE, axis=-1)


def after(value, *others):
    return lax.optimization_barrier((value,) + others)[0]


def narrow_all(x, axis):
    size = lax.axis_size("narrow")
    mine = lax.axis_index("narrow")
    if size == 2:
        other = lax.ppermute(x, "narrow", [(0, 1), (1, 0)])
        first = mine == 0
        return jnp.concatenate([jnp.where(first, x, other), jnp.where(first, other, x)], axis=axis)
    shape = list(x.shape)
    width = shape[axis]
    shape[axis] = width * size
    out = jnp.zeros(shape, x.dtype)
    for hop in range(size):
        got = x if hop == 0 else lax.ppermute(x, "narrow", [(i, (i + hop) % size) for i in range(size)])
        out = lax.dynamic_update_slice_in_dim(out, got, (mine - hop) % size * width, axis)
    return out


def swap(value, turn):
    wide = lax.axis_size("wide")
    narrow = lax.axis_size("narrow")
    pairs = []
    for i in range(wide):
        for j in range(narrow):
            pairs.append((i * narrow + j, (i ^ (1 if (j + turn) % 2 == 0 else 2)) * narrow + j))
    return lax.ppermute(value, ("wide", "narrow"), pairs)


def shifts(value):
    wide = lax.axis_size("wide")
    return [value] + [
        lax.ppermute(value, "wide", [(i, (i + 4 * hop) % wide) for i in range(wide)])
        for hop in range(1, wide // 4)
    ]


def positions(z_last):
    wide = lax.axis_size("wide")
    depth = wide // 4
    row_id = lax.axis_index("wide")
    odd = lax.axis_index("narrow") % 2
    z = (row_id // 4 - jnp.arange(depth, dtype=jnp.int32)) % depth
    flips = jnp.stack([0 * odd, 1 + odd, 2 - odd, 3 + 0 * odd])
    near = (row_id % 4) ^ flips
    if z_last:
        return (z[:, None] * 4 + near[None, :]).reshape(-1).astype(jnp.int32)
    return (z[None, :] * 4 + near[:, None]).reshape(-1).astype(jnp.int32)


def along_z(x, gate):
    return shifts(x if gate is None else after(x, gate))


def along_line(x, gate):
    wide = lax.axis_size("wide")
    depth = wide // 4
    z = lax.axis_index("wide") // 4
    up = down = x if gate is None else after(x, gate)
    ups, downs = [up], [down]
    for hop in range(1, depth):
        up = lax.ppermute(up, "wide", [(i, i + 4) for i in range(4 * (hop - 1), wide - 4)])
        down = lax.ppermute(down, "wide", [(i, i - 4) for i in range(4, wide - 4 * (hop - 1))])
        ups.append(up)
        downs.append(down)
    return ups, downs, [z >= hop for hop in range(depth)]


def line_pieces(ups, downs, below):
    depth = len(ups)
    return [ups[0]] + [jnp.where(below[k], ups[k], downs[depth - k]) for k in range(1, depth)]


def along_xy(pieces, gate):
    if gate is not None:
        held = lax.optimization_barrier(tuple(pieces) + (gate,))
        pieces = held[:-1]
    line = jnp.stack(pieces)
    return [line, swap(line, 0), swap(line, 1)]


def along_both(arrays, gate):
    near = arrays[1]
    return arrays + [swap(near if gate is None else after(near, *gate), 1)]


def product_body(plan, rows_n, steps_n, finish, *refs):
    place_ref, mask_ref = refs[0], refs[1]
    refs = refs[2:]
    row_refs = [refs[q * steps_n : (q + 1) * steps_n] for q in range(rows_n)]
    refs = refs[rows_n * steps_n :]
    count = sum(arrays for _, arrays, _ in plan)
    piece_refs, refs = refs[:count], refs[count:]
    if finish:
        diag_ref, out_ref, low_ref, lhs = refs
    else:
        out_ref, lhs = refs
    r = row_refs[0][0].shape[0]
    width = piece_refs[0].shape[-1]

    @pl.when(pl.program_id(0) == 0)
    def _():
        at = 0
        for g, (levels, arrays, each) in enumerate(plan):
            for i in range(arrays * each):
                start = pl.multiple_of(place_ref[g, i] * r, r)
                for j in levels:
                    for q in range(rows_n):
                        lhs[q * r : (q + 1) * r, at : at + r] = row_refs[q][j][:, pl.ds(start, r)]
                    at += r

    total = None
    at, base = 0, 0
    for levels, arrays, each in plan:
        depth = each * len(levels) * r
        for a in range(arrays):
            part = jnp.dot(
                lhs[:, at : at + depth],
                piece_refs[base + a][...].reshape(depth, width),
                preferred_element_type=F32,
            )
            total = part if total is None else total + part
            at += depth
        base += arrays
    here = pl.program_id(0)
    for q in range(rows_n):
        for t in range(width // TILE):
            keep = mask_ref[q, here * (width // TILE) + t] > 0
            cols = slice(t * TILE, (t + 1) * TILE)
            value = total[q * r : (q + 1) * r, cols]
            if finish:
                value = diag_ref[0, :, cols] - value
            else:
                value = -value
            value = jnp.where(keep, value, 0.0)
            if finish:
                out_ref[:, cols] = value
                low_ref[:, cols] = value.astype(BF)
            else:
                out_ref[q, :, cols] = value.astype(BF)


def product(rows, groups, mask, diag=None, shift=0):
    r = rows[0][0].shape[0]
    c = groups[0][2][0].shape[-1]
    rows_n, steps_n = len(rows), len(rows[0])
    if r % 128:
        total = 0.0
        for levels, place, arrays in groups:
            at = 0
            for array in arrays:
                each = array.shape[0]
                here = place[at : at + each]
                lhs = jnp.concatenate(
                    [
                        jnp.stack(
                            [jnp.take(row[j].reshape(r, -1, r), here, axis=1) for j in levels], axis=2
                        ).reshape(r, -1)
                        for row in rows
                    ],
                    axis=0,
                )
                total += jnp.dot(lhs, array.reshape(-1, c), preferred_element_type=F32)
                at += each
        total = total.reshape(rows_n, r, c)
        keep = jnp.repeat(mask, TILE, axis=1)[:, None, :] > 0
        if diag is None:
            return jnp.where(keep, -total, 0.0).astype(BF)
        level = diag[1]
        value = jnp.where(keep[0], diag[0][level, :, shift : shift + c] - total[0], 0.0)
        return value, value.astype(BF)
    width = TILE
    plan = tuple((tuple(levels), len(arrays), arrays[0].shape[0]) for levels, _, arrays in groups)
    place = jnp.stack([p for _, p, _ in groups])
    whole = pl.BlockSpec(memory_space=pltpu.VMEM)
    scalar = pl.BlockSpec(memory_space=pltpu.SMEM)
    pieces = [a for _, _, arrays in groups for a in arrays]
    piece_specs = [pl.BlockSpec(a.shape[:3] + (width,), lambda i: (0, 0, 0, i)) for a in pieces]
    flat = [x for row in rows for x in row]
    operands = [place, mask] + flat + pieces
    specs = [scalar, scalar] + [whole] * len(flat) + piece_specs
    if diag is None:
        outs = jax.ShapeDtypeStruct((rows_n, r, c), BF)
        out_specs = pl.BlockSpec((rows_n, r, width), lambda i: (0, 0, i))
    else:
        level = diag[1]
        skip = shift // width
        operands.append(diag[0])
        specs.append(pl.BlockSpec((1, r, width), lambda i: (level, 0, skip + i)))
        outs = (jax.ShapeDtypeStruct((r, c), F32), jax.ShapeDtypeStruct((r, c), BF))
        out_specs = (pl.BlockSpec((r, width), lambda i: (0, i)),) * 2
    deep = sum(len(levels) * arrays * each for levels, arrays, each in plan) * r
    return pl.pallas_call(
        functools.partial(product_body, plan, rows_n, steps_n, diag is not None),
        grid=(c // width,),
        in_specs=specs,
        out_specs=out_specs,
        out_shape=outs,
        scratch_shapes=[pltpu.VMEM((rows_n * r, deep), BF)],
        compiler_params=pltpu.CompilerParams(vmem_limit_bytes=VMEM),
        cost_estimate=pl.CostEstimate(
            flops=1, bytes_accessed=1, transcendentals=0
        ),
    )(*operands)


def slots_body(levels, wide, id_ref, own_ref, other_ref, slots_ref, full_ref):
    r, c = own_ref.shape[1:]
    part = r // 2
    half = wide // 2
    for n in range(2):

        @pl.when(id_ref[0] == n)
        def _():
            for h in range(2):
                ref = own_ref if h == n else other_ref
                for k in range(levels):
                    full_ref[k, :, h * c : (h + 1) * c] = ref[k]
                    for i in range(half):
                        slots_ref[h * half + i, k] = ref[k, n * part : (n + 1) * part, i * r : (i + 1) * r]


def make_slots(value):
    wide = lax.axis_size("wide")
    narrow = lax.axis_size("narrow")
    l, r, c = value.shape
    if narrow != 2 or r % 128:
        full = narrow_all(value, 2)
        part = r // narrow
        mine = lax.dynamic_slice_in_dim(full, lax.axis_index("narrow") * part, part, 1)
        return mine.reshape(l, part, wide, r).transpose(2, 0, 1, 3), full
    other = lax.ppermute(value, "narrow", [(0, 1), (1, 0)])
    whole = pl.BlockSpec(memory_space=pltpu.VMEM)
    return pl.pallas_call(
        functools.partial(slots_body, l, wide),
        in_specs=[pl.BlockSpec(memory_space=pltpu.SMEM), whole, whole],
        out_specs=(whole, whole),
        out_shape=(
            jax.ShapeDtypeStruct((wide, l, r // 2, r), BF),
            jax.ShapeDtypeStruct((l, r, 2 * c), BF),
        ),
        compiler_params=pltpu.CompilerParams(vmem_limit_bytes=VMEM),
        cost_estimate=pl.CostEstimate(flops=1, bytes_accessed=1, transcendentals=0),
    )(lax.axis_index("narrow").astype(jnp.int32).reshape(1), value, other)


def turn_body(levels, wide, id_ref, own_ref, other_ref, out_ref):
    r = out_ref.shape[1]
    for n in range(2):

        @pl.when(id_ref[0] == n)
        def _():
            first, second = (own_ref, other_ref) if n == 0 else (other_ref, own_ref)
            for k in range(levels):
                for w in range(wide):
                    block = jnp.concatenate([first[w, k], second[w, k]], axis=0)
                    out_ref[k, :, w * r : (w + 1) * r] = block.T


def mirrored(got, full):
    wide = lax.axis_size("wide")
    narrow = lax.axis_size("narrow")
    l, r, cols = full.shape
    if narrow != 2 or r % 128:
        return narrow_all(got, 2).transpose(1, 3, 0, 2).reshape(l, r, cols)
    other = lax.ppermute(got, "narrow", [(0, 1), (1, 0)])
    whole = pl.BlockSpec(memory_space=pltpu.VMEM)
    return pl.pallas_call(
        functools.partial(turn_body, l, wide),
        in_specs=[pl.BlockSpec(memory_space=pltpu.SMEM), whole, whole],
        out_specs=whole,
        out_shape=jax.ShapeDtypeStruct((l, r, cols), BF),
        compiler_params=pltpu.CompilerParams(vmem_limit_bytes=VMEM),
        cost_estimate=pl.CostEstimate(flops=1, bytes_accessed=1, transcendentals=0),
    )(lax.axis_index("narrow").astype(jnp.int32).reshape(1), got, other)


SRC, POS, HELD, OWN, KEEP = 0, 16, 24, 40, 48
WIDTHS = {2: (4, 2), 3: (4, 2, 1)}


def table_body(id_ref, parent_ref, node_ref, structure_ref, out_ref):
    core, row = id_ref[0], id_ref[1]
    for i in range(out_ref.shape[0]):
        out_ref[i] = jnp.int32(0)
    one, none = jnp.int32(1), jnp.int32(0)
    nodes = [[node_ref[k, t] for t in range(LT)] for k in range(LEV)]
    above = [[parent_ref[nodes[k][t]] for t in range(LT)] for k in range(LEV)]
    left = nodes[1][0]
    key1 = [jnp.where(nodes[1][t] == left, none, one) for t in range(LT)]

    def second(k, t):
        found = none
        for u in range(LT):
            less = (above[k][u] == above[k][t]) & (nodes[k][u] < nodes[k][t])
            found = jnp.where(less, one, found)
        return found

    key2 = [jnp.where(above[2][t] == left, none, 2 * one) + second(2, t) for t in range(LT)]
    for t in range(LT):
        again = none
        for u in range(t):
            again = jnp.where(nodes[2][u] == nodes[2][t], one, again)
        place = again * 4 + key2[t]
        out_ref[SRC + t] = place
        out_ref[HELD + place] = jnp.int32(t)
        upper = none
        for u in range(LT):
            upper = jnp.where(nodes[2][u] == above[3][t], key2[u], upper)
        place = second(3, t) * 4 + upper
        out_ref[SRC + LT + t] = place
        out_ref[HELD + LT + place] = jnp.int32(t)
        rank = none
        for u in range(t):
            rank = rank + jnp.where(key1[u] == key1[t], one, none)
        out_ref[POS + key1[t] * 4 + rank] = jnp.int32(t)

        @pl.when(row == t)
        def _():
            out_ref[OWN] = key1[t]
            out_ref[OWN + 1] = key2[t]
            out_ref[OWN + 2] = out_ref[SRC + LT + t] % 4

    for m in (2, 3):
        for k in range(m):
            for i in range(WIDTHS[m][k]):
                q = i
                if k == 1:
                    q = out_ref[OWN] * 2 + i
                if k == 2:
                    q = out_ref[OWN + 1]
                tile = out_ref[HELD + (m - 2) * LT + core * 4 + q]
                at = KEEP + (m - 2) * 16 + k * 4 + i
                out_ref[at] = structure_ref[node_ref[m, tile], k, row]
                out_ref[at + 32] = tile


def make_table(parent, tile_node, structure, row_tile):
    ids = jnp.stack([lax.axis_index("narrow"), row_tile]).astype(jnp.int32)
    return pl.pallas_call(
        table_body,
        in_specs=[pl.BlockSpec(memory_space=pltpu.SMEM)] * 4,
        out_specs=pl.BlockSpec(memory_space=pltpu.SMEM),
        out_shape=jax.ShapeDtypeStruct((128,), jnp.int32),
    )(ids, parent, tile_node, structure)


PAIRS = ((0, 2), (1, 2), (0, 3), (1, 3), (2, 3))


def pack_body(id_ref, table_ref, own_ref, other_ref, two_ref, three_ref):
    half = LT // 2
    for b, (k, m) in enumerate(PAIRS):
        out = two_ref if m == 2 else three_ref
        base = sum(WIDTHS[m][:k])
        for i in range(WIDTHS[m][k]):
            at = KEEP + (m - 2) * 16 + k * 4 + i
            tile = table_ref[at + 32]
            keep = table_ref[at] > 0
            mine = tile // half == id_ref[0]
            start = pl.multiple_of(tile % half * TILE, TILE)
            cols = slice((base + i) * TILE, (base + i + 1) * TILE)

            @pl.when(keep & mine)
            def _():
                out[:, cols] = own_ref[b, :, pl.ds(start, TILE)]

            @pl.when(keep & jnp.logical_not(mine))
            def _():
                out[:, cols] = other_ref[b, :, pl.ds(start, TILE)]

            @pl.when(jnp.logical_not(keep))
            def _():
                out[:, cols] = jnp.zeros((out.shape[0], TILE), BF)


def packed(factor, table):
    r = factor.shape[1]
    own = jnp.stack([factor[k, :, m, :] for k, m in PAIRS])
    other = lax.ppermute(own, "narrow", [(0, 1), (1, 0)])
    whole = pl.BlockSpec(memory_space=pltpu.VMEM)
    scalar = pl.BlockSpec(memory_space=pltpu.SMEM)
    return pl.pallas_call(
        pack_body,
        in_specs=[scalar, scalar, whole, whole],
        out_specs=(whole,) * 2,
        out_shape=tuple(jax.ShapeDtypeStruct((r, sum(WIDTHS[m]) * TILE), BF) for m in (2, 3)),
        compiler_params=pltpu.CompilerParams(vmem_limit_bytes=VMEM),
        cost_estimate=pl.CostEstimate(flops=1, bytes_accessed=1, transcendentals=0),
    )(lax.axis_index("narrow").astype(jnp.int32).reshape(1), table, own, other)


def sparse_body(level, shapes, mirror, table_ref, place_ref, *refs):
    row_refs, refs = refs[: len(shapes)], refs[len(shapes) :]
    out_ref, lhs, rest = refs[-3:]
    piece_refs = refs[:-3]
    r = row_refs[0].shape[-2]
    span = LT * TILE
    per = TILE // r
    q = pl.program_id(0)

    @pl.when(q == 0)
    def _():
        for ref, (_, many, at) in zip(row_refs, shapes, strict=True):
            for p in range(many):
                row, j = at[p]
                block = ref[p] if len(ref.shape) == 3 else ref[...]
                lhs[row * r : (row + 1) * r, j * span : (j + 1) * span] = block
        each = piece_refs[0].shape[0]
        for a in range(4):
            for i in range(each):
                rest[place_ref[a * each + i]] = piece_refs[a][i]

    if mirror:
        q = table_ref[OWN + level - 1]
    block = rest[:, :, pl.ds(pl.multiple_of(q * TILE, TILE), TILE)]
    total = jnp.dot(lhs[:, :span], block.reshape(span, TILE), preferred_element_type=F32)
    for j in range(1, level):
        for i in range(4 // j):
            if j == 1:
                tile = table_ref[POS + q // 2 * 4 + i]
            else:
                tile = table_ref[HELD + i * 4 + q]
            start = pl.multiple_of(j * span + tile * TILE, TILE)
            if j == 1:
                block = rest[pl.ds(tile * per, per), :, pl.ds(pl.multiple_of((4 + q % 2) * TILE, TILE), TILE)]
            else:
                block = rest[pl.ds(tile * per, per), :, 6 * TILE : 7 * TILE]
            total += jnp.dot(
                lhs[:, pl.ds(start, TILE)], block.reshape(TILE, TILE), preferred_element_type=F32
            )
    if mirror:
        out_ref[...] = total
    else:
        for p in range(level):
            value = -total[p * r : (p + 1) * r]
            if p == 1:
                value = jnp.where(table_ref[OWN] == q // 2, value, 0.0)
            if p == 2:
                value = jnp.where(table_ref[OWN + 1] == q, value, 0.0)
            out_ref[p] = value.astype(BF)


def sparse_product(level, table, place, rows, rest, mirror):
    wide = lax.axis_size("wide")
    r = rows[0][0].shape[-2]
    rows_n = 1 if mirror else level

    whole = pl.BlockSpec(memory_space=pltpu.VMEM)
    flat = [array for array, _ in rows]
    shapes = tuple((0, len(at), at) for _, at in rows)
    specs = [pl.BlockSpec(memory_space=pltpu.SMEM)] + [whole] * len(flat)
    operands = [table, place] + flat
    specs += [whole] * len(rest)
    operands += rest
    if mirror:
        shape = jax.ShapeDtypeStruct((r, TILE), F32)
        out_spec = pl.BlockSpec((r, TILE), lambda i, t: (0, 0))
    else:
        shape = jax.ShapeDtypeStruct((rows_n, r, 4 * TILE), BF)
        out_spec = pl.BlockSpec((rows_n, r, TILE), lambda i, t: (0, 0, i))
    return pl.pallas_call(
        functools.partial(sparse_body, level, shapes, mirror),
        grid_spec=pltpu.PrefetchScalarGridSpec(
            num_scalar_prefetch=1,
            grid=(1 if mirror else 4,),
            in_specs=specs,
            out_specs=out_spec,
            scratch_shapes=[
                pltpu.VMEM((rows_n * r, level * LT * TILE), BF),
                pltpu.VMEM((wide, r, rest[0].shape[-1]), BF),
            ],
        ),
        out_shape=shape,
        compiler_params=pltpu.CompilerParams(vmem_limit_bytes=VMEM),
        cost_estimate=pl.CostEstimate(flops=1, bytes_accessed=1, transcendentals=0),
    )(*operands)


def place_body(level, levels, id_ref, table_ref, own_ref, other_ref, slots_ref, full_ref):
    r = own_ref.shape[1]
    part = r // 2
    per = TILE // r
    me = id_ref[0]
    first = pl.multiple_of(me * part, part)
    for c in range(LT):
        source = table_ref[SRC + (level - 2) * LT + c]
        start = pl.multiple_of(source % 4 * TILE, TILE)

        def put(ref):
            for k in range(levels):
                full_ref[k, :, c * TILE : (c + 1) * TILE] = ref[k, :, pl.ds(start, TILE)]
                for i in range(per):
                    at = pl.multiple_of(start + i * r, r)
                    slots_ref[c * per + i, k] = ref[k, pl.ds(first, part), pl.ds(at, r)]

        @pl.when(source // 4 == me)
        def _():
            put(own_ref)

        @pl.when(source // 4 != me)
        def _():
            put(other_ref)


def place_slots(level, table, value):
    wide = lax.axis_size("wide")
    l, r, c = value.shape
    other = lax.ppermute(value, "narrow", [(0, 1), (1, 0)])
    whole = pl.BlockSpec(memory_space=pltpu.VMEM)
    scalar = pl.BlockSpec(memory_space=pltpu.SMEM)
    return pl.pallas_call(
        functools.partial(place_body, level, l),
        in_specs=[scalar, scalar, whole, whole],
        out_specs=(whole, whole),
        out_shape=(
            jax.ShapeDtypeStruct((wide, l, r // 2, r), BF),
            jax.ShapeDtypeStruct((l, r, 2 * c), BF),
        ),
        compiler_params=pltpu.CompilerParams(vmem_limit_bytes=VMEM),
        cost_estimate=pl.CostEstimate(flops=1, bytes_accessed=1, transcendentals=0),
    )(lax.axis_index("narrow").astype(jnp.int32).reshape(1), table, value, other)


def diag_body(level, id_ref, table_ref, own_ref, other_ref, diag_ref, out_ref, low_ref):
    me, row = id_ref[0], id_ref[1]
    half = LT // 2
    base = SRC + (level - 2) * LT
    for c in range(LT):
        source = table_ref[base + c]
        same = source % 4 == table_ref[base + row] % 4
        if level == 3:
            same = row == c
        cols = slice(c * TILE, (c + 1) * TILE)
        inner = jnp.where(source // 4 == me, own_ref[...], other_ref[...])
        value = jnp.where(same, diag_ref[:, cols] - inner, 0.0)
        low_ref[:, cols] = value.astype(BF)

        @pl.when(me == c // half)
        def _():
            out_ref[:, (c % half) * TILE : (c % half + 1) * TILE] = value


def diag_block(level, table, inner, diag, row_tile):
    r, span = diag.shape
    other = lax.ppermute(inner, "narrow", [(0, 1), (1, 0)])
    ids = jnp.stack([lax.axis_index("narrow"), row_tile]).astype(jnp.int32)
    whole = pl.BlockSpec(memory_space=pltpu.VMEM)
    scalar = pl.BlockSpec(memory_space=pltpu.SMEM)
    return pl.pallas_call(
        functools.partial(diag_body, level),
        in_specs=[scalar, scalar, whole, whole, whole],
        out_specs=(whole, whole),
        out_shape=(jax.ShapeDtypeStruct((r, span // 2), F32), jax.ShapeDtypeStruct((r, span), BF)),
        compiler_params=pltpu.CompilerParams(vmem_limit_bytes=VMEM),
        cost_estimate=pl.CostEstimate(flops=1, bytes_accessed=1, transcendentals=0),
    )(ids, table, inner, other, diag)


def upper_body(id_ref, first_ref, *refs):
    news, turns, diags, out_ref = refs[0:3], refs[3:5], refs[5:7], refs[7]
    for k in range(LEV - 1):
        for m in range(LEV):
            if m == k:
                value = first_ref[0] if k == 0 else diags[k - 1][...]
            elif m > k:
                value = news[m - 1][k].astype(F32)
            else:
                value = turns[k - 1][m].astype(F32)
            out_ref[k, :, m, :] = value


def lower_body(id_ref, turn_ref, diag_ref, held_ref, out_ref):
    for m in range(LEV - 1):
        out_ref[0, :, m, :] = turn_ref[m].astype(F32)
    out_ref[0, :, LEV - 1, :] = diag_ref[...]


def upper_rows(diag_inverse, news, turns, diags):
    r, c = diag_inverse.shape[1:]
    step = min(r, 32)
    shape = jax.ShapeDtypeStruct((LEV, r, LEV, c), F32)
    specs = [pl.BlockSpec((1, step, c), lambda i, n: (0, i, 0))]
    specs += [pl.BlockSpec((m, step, c), lambda i, n: (0, i, n[0])) for m in range(1, LEV)]
    specs += [pl.BlockSpec((k, step, c), lambda i, n: (0, i, n[0])) for k in range(1, LEV - 1)]
    specs += [pl.BlockSpec((step, c), lambda i, n: (i, 0)) for k in range(1, LEV - 1)]
    return pl.pallas_call(
        upper_body,
        grid_spec=pltpu.PrefetchScalarGridSpec(
            num_scalar_prefetch=1,
            grid=(r // step,),
            in_specs=specs,
            out_specs=pl.BlockSpec((LEV - 1, step, LEV, c), lambda i, n: (0, i, 0, 0)),
        ),
        out_shape=shape,
        compiler_params=pltpu.CompilerParams(vmem_limit_bytes=VMEM),
        cost_estimate=pl.CostEstimate(flops=0, bytes_accessed=40 * 2**20, transcendentals=0),
    )(lax.axis_index("narrow").astype(jnp.int32).reshape(1), diag_inverse, *news, *turns, *diags)


def lower_rows(turn, diag, held):
    r, c = diag.shape
    step = min(r, 32)
    return pl.pallas_call(
        lower_body,
        grid_spec=pltpu.PrefetchScalarGridSpec(
            num_scalar_prefetch=1,
            grid=(r // step,),
            in_specs=[
                pl.BlockSpec((LEV - 1, step, c), lambda i, n: (0, i, n[0])),
                pl.BlockSpec((step, c), lambda i, n: (i, 0)),
                pl.BlockSpec(memory_space=pl.ANY),
            ],
            out_specs=pl.BlockSpec((1, step, LEV, c), lambda i, n: (LEV - 1, i, 0, 0)),
        ),
        out_shape=jax.ShapeDtypeStruct(held.shape, F32),
        input_output_aliases={3: 0},
        compiler_params=pltpu.CompilerParams(vmem_limit_bytes=VMEM),
        cost_estimate=pl.CostEstimate(flops=0, bytes_accessed=1, transcendentals=0),
    )(lax.axis_index("narrow").astype(jnp.int32).reshape(1), turn, diag, held)


def local(factor, diag_inverse, parent, tile_node, structure):
    row_count = factor.shape[1]
    col_count = factor.shape[3]
    col_tiles = col_count // TILE
    row_id = lax.axis_index("wide")
    col_id = lax.axis_index("narrow")
    high = lax.Precision.HIGHEST
    reach = ancestors(parent)
    node_hot = (tile_node[:, :, None] == jnp.arange(M, dtype=jnp.int32)[None, None, :]).astype(
        jnp.float32
    )
    row_pos = row_id * row_count // TILE
    pos_hot = (jnp.arange(LT, dtype=jnp.int32) == row_pos).astype(jnp.float32)
    row_hot = jnp.einsum("t,ltm->lm", pos_hot, node_hot, precision=high)
    col_sel = (
        jnp.arange(LT, dtype=jnp.int32)[None, :]
        == (col_id * col_tiles + jnp.arange(col_tiles, dtype=jnp.int32))[:, None]
    ).astype(jnp.float32)
    col_hot = jnp.einsum("jt,ltm->ljm", col_sel, node_hot, precision=high)
    tile_above = jnp.einsum("ra,ba,cjb->rcj", row_hot, reach, col_hot, precision=high)
    tile_same = jnp.einsum("lm,ljm->lj", row_hot, col_hot, precision=high)
    struct_row = jnp.einsum("mlt,t->ml", structure.astype(jnp.float32), pos_hot, precision=high)
    tile_struct = jnp.einsum("cjm,mr->rcj", col_hot, struct_row, precision=high)
    above = (tile_above > 0.5).astype(jnp.int32)
    same = (tile_same > 0.5).astype(jnp.int32)

    def masked(k, m):
        return (factor[k, :, m, :] * spread(tile_struct[k, m])[None, :].astype(BF))[None]

    place = positions(False)

    def panel_of(level):
        return jnp.concatenate([masked(k, level) for k in range(level)], axis=0)

    wide = lax.axis_size("wide")
    whole_place = jnp.arange(wide, dtype=jnp.int32)
    compact = lax.axis_size("narrow") == 2 and row_count % 128 == 0 and TILE % row_count == 0
    first = along_z(panel_of(1), None)
    if compact:
        table = make_table(parent, tile_node, structure, row_pos)
        shards = packed(factor, table)
        wide_diag = {m: narrow_all(diag_inverse[m], 1) for m in (2, 3)}
    else:
        panels = {m: lax.all_gather(panel_of(m), "wide", axis=0) for m in (2, 3)}
    one = along_xy(first, None)
    if compact:
        second = along_z(after(shards[0], one[0]), None)
    one = along_both(one, (one[2],) + tuple(second) if compact else None)

    held = {}
    rows = {0: [(narrow_all(diag_inverse[0].astype(BF), 1), ((0, 0),))]}
    news, turns, diags = [], [], []
    rest = []
    for level in range(1, LEV):
        packed_here = compact and level > 1
        if packed_here:
            known = [part for k in range(level) for part in rows[k]] + [held[m] for m in range(1, level)]
            if level == 2:
                held_line = lax.optimization_barrier(tuple(third[0] + third[1]) + (diags[0],))
                depth = len(third[0])
                ahead = along_xy(line_pieces(held_line[:depth], held_line[depth:-1], third[2]), None)
            value = sparse_product(level, table, place, known, rest, False)
            slots, full = place_slots(level, table, value)
        else:
            if level == 1:
                groups = [((0,), place, one)]
                known = [[rows[0][0][0]]]
            else:
                groups = [(tuple(range(level)), whole_place, [panels[level]])]
                known = []
                for k in range(level):
                    by_level = {}
                    for array, at in rows[k] + [held[m] for m in range(1, level)]:
                        for p, (row, j) in enumerate(at):
                            if row == k:
                                by_level[j] = array[p] if array.ndim == 3 else array
                    known.append([by_level[j] for j in range(level)])
            value = product(known, groups, above[:level, level])
            if compact:
                ahead = along_xy(second, value)
                third = along_line(after(shards[1], ahead[0]), None)
            slots, full = make_slots(value)
        news.append(full)
        held[level] = (full, tuple((k, level) for k in range(level)))
        if level == LEV - 1:
            out = upper_rows(diag_inverse, news, turns, diags)
        got = lax.all_to_all(slots, "wide", split_axis=0, concat_axis=0, tiled=True)
        if level == LEV - 1:
            got = after(got, out)
        now = rest
        if compact and level < LEV - 1:
            if level == 1:
                rest = along_both(ahead, (got, ahead[2]) + tuple(third[0][1:] + third[1][1:]))
                got = after(got, ahead[1], ahead[2])
            else:
                rest = along_both(ahead, (slots, ahead[2]))
                got = after(got, ahead[1], ahead[2])
        turn = mirrored(got, full)
        turns.append(turn)
        rows[level] = [(turn, tuple((level, j) for j in range(level)))]
        if packed_here:
            here = [(turn, tuple((0, j) for j in range(level)))]
            inner = sparse_product(level, table, place, here, now, True)
            done, whole_low = diag_block(level, table, inner, wide_diag[level], row_pos)
        else:
            known = [[turn[k] for k in range(level)]]
            done, low = product(known, groups, same[level : level + 1], (diag_inverse, level))
            whole_low = narrow_all(low, 1) if level < LEV - 1 else None
        diags.append(done)
        if level < LEV - 1:
            rows[level].append((whole_low, ((level, level),)))
    return lower_rows(turns[-1], diags[-1], out)


def solution(mesh):
    return jax.shard_map(
        local,
        mesh=mesh,
        in_specs=(P(None, "wide", None, "narrow"), P(None, "wide", "narrow"), P(), P(), P()),
        out_specs=P(None, "wide", None, "narrow"),
        check_vma=False,
    )
```

```python
import functools

import jax
import jax.numpy as jnp
from jax import lax
from jax.experimental import pallas as pl
from jax.experimental.pallas import tpu as pltpu
from jax.sharding import PartitionSpec as P

LEV = 4
TILE = 256
LT = 8
M = 15
BF = jnp.bfloat16
F32 = jnp.float32
VMEM = 56 * 1024 * 1024


def ancestors(parent):
    node_ids = jnp.arange(M, dtype=jnp.int32)
    step_mat = (parent[:, None] == node_ids[None, :]).astype(jnp.float32)
    power_mat = step_mat
    reach = step_mat
    for hop_count in range(LEV - 2):
        power_mat = jnp.dot(power_mat, step_mat, precision=lax.Precision.HIGHEST)
        reach = reach + power_mat
    return reach


def spread(mask_tile):
    return jnp.repeat(mask_tile, TILE, axis=-1)


def after(value, *others):
    return lax.optimization_barrier((value,) + others)[0]


def narrow_all(x, axis):
    size = lax.axis_size("narrow")
    mine = lax.axis_index("narrow")
    if size == 2:
        other = lax.ppermute(x, "narrow", [(0, 1), (1, 0)])
        first = mine == 0
        return jnp.concatenate([jnp.where(first, x, other), jnp.where(first, other, x)], axis=axis)
    shape = list(x.shape)
    width = shape[axis]
    shape[axis] = width * size
    out = jnp.zeros(shape, x.dtype)
    for hop in range(size):
        got = x if hop == 0 else lax.ppermute(x, "narrow", [(i, (i + hop) % size) for i in range(size)])
        out = lax.dynamic_update_slice_in_dim(out, got, (mine - hop) % size * width, axis)
    return out


def swap(value, turn):
    wide = lax.axis_size("wide")
    narrow = lax.axis_size("narrow")
    pairs = []
    for i in range(wide):
        for j in range(narrow):
            pairs.append((i * narrow + j, (i ^ (1 if (j + turn) % 2 == 0 else 2)) * narrow + j))
    return lax.ppermute(value, ("wide", "narrow"), pairs)


def shifts(value):
    wide = lax.axis_size("wide")
    return [value] + [
        lax.ppermute(value, "wide", [(i, (i + 4 * hop) % wide) for i in range(wide)])
        for hop in range(1, wide // 4)
    ]


def positions(z_last):
    wide = lax.axis_size("wide")
    depth = wide // 4
    row_id = lax.axis_index("wide")
    odd = lax.axis_index("narrow") % 2
    z = (row_id // 4 - jnp.arange(depth, dtype=jnp.int32)) % depth
    flips = jnp.stack([0 * odd, 1 + odd, 2 - odd, 3 + 0 * odd])
    near = (row_id % 4) ^ flips
    if z_last:
        return (z[:, None] * 4 + near[None, :]).reshape(-1).astype(jnp.int32)
    return (z[None, :] * 4 + near[:, None]).reshape(-1).astype(jnp.int32)


def along_z(x, gate):
    return shifts(x if gate is None else after(x, gate))


def along_line(x, gate):
    wide = lax.axis_size("wide")
    depth = wide // 4
    z = lax.axis_index("wide") // 4
    up = down = x if gate is None else after(x, gate)
    ups, downs = [up], [down]
    for hop in range(1, depth):
        up = lax.ppermute(up, "wide", [(i, i + 4) for i in range(4 * (hop - 1), wide - 4)])
        down = lax.ppermute(down, "wide", [(i, i - 4) for i in range(4, wide - 4 * (hop - 1))])
        ups.append(up)
        downs.append(down)
    return ups, downs, [z >= hop for hop in range(depth)]


def line_pieces(ups, downs, below):
    depth = len(ups)
    return [ups[0]] + [jnp.where(below[k], ups[k], downs[depth - k]) for k in range(1, depth)]


def along_xy(pieces, gate):
    if gate is not None:
        held = lax.optimization_barrier(tuple(pieces) + (gate,))
        pieces = held[:-1]
    line = jnp.stack(pieces)
    return [line, swap(line, 0), swap(line, 1)]


def along_both(arrays, gate):
    near = arrays[1]
    return arrays + [swap(near if gate is None else after(near, *gate), 1)]


def product_body(plan, rows_n, steps_n, finish, *refs):
    place_ref, mask_ref = refs[0], refs[1]
    refs = refs[2:]
    row_refs = [refs[q * steps_n : (q + 1) * steps_n] for q in range(rows_n)]
    refs = refs[rows_n * steps_n :]
    count = sum(arrays for _, arrays, _ in plan)
    piece_refs, refs = refs[:count], refs[count:]
    if finish:
        diag_ref, out_ref, low_ref, lhs = refs
    else:
        out_ref, lhs = refs
    r = row_refs[0][0].shape[0]
    width = piece_refs[0].shape[-1]

    @pl.when(pl.program_id(0) == 0)
    def _():
        at = 0
        for g, (levels, arrays, each) in enumerate(plan):
            for i in range(arrays * each):
                start = pl.multiple_of(place_ref[g, i] * r, r)
                for j in levels:
                    for q in range(rows_n):
                        lhs[q * r : (q + 1) * r, at : at + r] = row_refs[q][j][:, pl.ds(start, r)]
                    at += r

    total = None
    at, base = 0, 0
    for levels, arrays, each in plan:
        depth = each * len(levels) * r
        for a in range(arrays):
            part = jnp.dot(
                lhs[:, at : at + depth],
                piece_refs[base + a][...].reshape(depth, width),
                preferred_element_type=F32,
            )
            total = part if total is None else total + part
            at += depth
        base += arrays
    here = pl.program_id(0)
    for q in range(rows_n):
        for t in range(width // TILE):
            keep = mask_ref[q, here * (width // TILE) + t] > 0
            cols = slice(t * TILE, (t + 1) * TILE)
            value = total[q * r : (q + 1) * r, cols]
            if finish:
                value = diag_ref[0, :, cols] - value
            else:
                value = -value
            value = jnp.where(keep, value, 0.0)
            if finish:
                out_ref[:, cols] = value
                low_ref[:, cols] = value.astype(BF)
            else:
                out_ref[q, :, cols] = value.astype(BF)


def product(rows, groups, mask, diag=None, shift=0):
    r = rows[0][0].shape[0]
    c = groups[0][2][0].shape[-1]
    rows_n, steps_n = len(rows), len(rows[0])
    if r % 128:
        total = 0.0
        for levels, place, arrays in groups:
            at = 0
            for array in arrays:
                each = array.shape[0]
                here = place[at : at + each]
                lhs = jnp.concatenate(
                    [
                        jnp.stack(
                            [jnp.take(row[j].reshape(r, -1, r), here, axis=1) for j in levels], axis=2
                        ).reshape(r, -1)
                        for row in rows
                    ],
                    axis=0,
                )
                total += jnp.dot(lhs, array.reshape(-1, c), preferred_element_type=F32)
                at += each
        total = total.reshape(rows_n, r, c)
        keep = jnp.repeat(mask, TILE, axis=1)[:, None, :] > 0
        if diag is None:
            return jnp.where(keep, -total, 0.0).astype(BF)
        level = diag[1]
        value = jnp.where(keep[0], diag[0][level, :, shift : shift + c] - total[0], 0.0)
        return value, value.astype(BF)
    width = TILE
    plan = tuple((tuple(levels), len(arrays), arrays[0].shape[0]) for levels, _, arrays in groups)
    place = jnp.stack([p for _, p, _ in groups])
    whole = pl.BlockSpec(memory_space=pltpu.VMEM)
    scalar = pl.BlockSpec(memory_space=pltpu.SMEM)
    pieces = [a for _, _, arrays in groups for a in arrays]
    piece_specs = [pl.BlockSpec(a.shape[:3] + (width,), lambda i: (0, 0, 0, i)) for a in pieces]
    flat = [x for row in rows for x in row]
    operands = [place, mask] + flat + pieces
    specs = [scalar, scalar] + [whole] * len(flat) + piece_specs
    if diag is None:
        outs = jax.ShapeDtypeStruct((rows_n, r, c), BF)
        out_specs = pl.BlockSpec((rows_n, r, width), lambda i: (0, 0, i))
    else:
        level = diag[1]
        skip = shift // width
        operands.append(diag[0])
        specs.append(pl.BlockSpec((1, r, width), lambda i: (level, 0, skip + i)))
        outs = (jax.ShapeDtypeStruct((r, c), F32), jax.ShapeDtypeStruct((r, c), BF))
        out_specs = (pl.BlockSpec((r, width), lambda i: (0, i)),) * 2
    deep = sum(len(levels) * arrays * each for levels, arrays, each in plan) * r
    return pl.pallas_call(
        functools.partial(product_body, plan, rows_n, steps_n, diag is not None),
        grid=(c // width,),
        in_specs=specs,
        out_specs=out_specs,
        out_shape=outs,
        scratch_shapes=[pltpu.VMEM((rows_n * r, deep), BF)],
        compiler_params=pltpu.CompilerParams(vmem_limit_bytes=VMEM),
        cost_estimate=pl.CostEstimate(
            flops=1, bytes_accessed=1, transcendentals=0
        ),
    )(*operands)


def slots_body(levels, wide, id_ref, own_ref, other_ref, slots_ref, full_ref):
    r, c = own_ref.shape[1:]
    part = r // 2
    half = wide // 2
    for n in range(2):

        @pl.when(id_ref[0] == n)
        def _():
            for h in range(2):
                ref = own_ref if h == n else other_ref
                for k in range(levels):
                    full_ref[k, :, h * c : (h + 1) * c] = ref[k]
                    for i in range(half):
                        slots_ref[h * half + i, k] = ref[k, n * part : (n + 1) * part, i * r : (i + 1) * r]


def make_slots(value):
    wide = lax.axis_size("wide")
    narrow = lax.axis_size("narrow")
    l, r, c = value.shape
    if narrow != 2 or r % 128:
        full = narrow_all(value, 2)
        part = r // narrow
        mine = lax.dynamic_slice_in_dim(full, lax.axis_index("narrow") * part, part, 1)
        return mine.reshape(l, part, wide, r).transpose(2, 0, 1, 3), full
    other = lax.ppermute(value, "narrow", [(0, 1), (1, 0)])
    whole = pl.BlockSpec(memory_space=pltpu.VMEM)
    return pl.pallas_call(
        functools.partial(slots_body, l, wide),
        in_specs=[pl.BlockSpec(memory_space=pltpu.SMEM), whole, whole],
        out_specs=(whole, whole),
        out_shape=(
            jax.ShapeDtypeStruct((wide, l, r // 2, r), BF),
            jax.ShapeDtypeStruct((l, r, 2 * c), BF),
        ),
        compiler_params=pltpu.CompilerParams(vmem_limit_bytes=VMEM),
        cost_estimate=pl.CostEstimate(flops=1, bytes_accessed=1, transcendentals=0),
    )(lax.axis_index("narrow").astype(jnp.int32).reshape(1), value, other)


def turn_body(levels, wide, id_ref, own_ref, other_ref, out_ref):
    r = out_ref.shape[1]
    for n in range(2):

        @pl.when(id_ref[0] == n)
        def _():
            first, second = (own_ref, other_ref) if n == 0 else (other_ref, own_ref)
            for k in range(levels):
                for w in range(wide):
                    block = jnp.concatenate([first[w, k], second[w, k]], axis=0)
                    out_ref[k, :, w * r : (w + 1) * r] = block.T


def mirrored(got, full):
    wide = lax.axis_size("wide")
    narrow = lax.axis_size("narrow")
    l, r, cols = full.shape
    if narrow != 2 or r % 128:
        return narrow_all(got, 2).transpose(1, 3, 0, 2).reshape(l, r, cols)
    other = lax.ppermute(got, "narrow", [(0, 1), (1, 0)])
    whole = pl.BlockSpec(memory_space=pltpu.VMEM)
    return pl.pallas_call(
        functools.partial(turn_body, l, wide),
        in_specs=[pl.BlockSpec(memory_space=pltpu.SMEM), whole, whole],
        out_specs=whole,
        out_shape=jax.ShapeDtypeStruct((l, r, cols), BF),
        compiler_params=pltpu.CompilerParams(vmem_limit_bytes=VMEM),
        cost_estimate=pl.CostEstimate(flops=1, bytes_accessed=1, transcendentals=0),
    )(lax.axis_index("narrow").astype(jnp.int32).reshape(1), got, other)


SRC, POS, HELD, OWN, KEEP = 0, 16, 24, 40, 48
WIDTHS = {2: (4, 2), 3: (4, 2, 1)}


def table_body(id_ref, parent_ref, node_ref, structure_ref, out_ref):
    core, row = id_ref[0], id_ref[1]
    for i in range(out_ref.shape[0]):
        out_ref[i] = jnp.int32(0)
    one, none = jnp.int32(1), jnp.int32(0)
    nodes = [[node_ref[k, t] for t in range(LT)] for k in range(LEV)]
    above = [[parent_ref[nodes[k][t]] for t in range(LT)] for k in range(LEV)]
    left = nodes[1][0]
    key1 = [jnp.where(nodes[1][t] == left, none, one) for t in range(LT)]

    def second(k, t):
        found = none
        for u in range(LT):
            less = (above[k][u] == above[k][t]) & (nodes[k][u] < nodes[k][t])
            found = jnp.where(less, one, found)
        return found

    key2 = [jnp.where(above[2][t] == left, none, 2 * one) + second(2, t) for t in range(LT)]
    for t in range(LT):
        again = none
        for u in range(t):
            again = jnp.where(nodes[2][u] == nodes[2][t], one, again)
        place = again * 4 + key2[t]
        out_ref[SRC + t] = place
        out_ref[HELD + place] = jnp.int32(t)
        upper = none
        for u in range(LT):
            upper = jnp.where(nodes[2][u] == above[3][t], key2[u], upper)
        place = second(3, t) * 4 + upper
        out_ref[SRC + LT + t] = place
        out_ref[HELD + LT + place] = jnp.int32(t)
        rank = none
        for u in range(t):
            rank = rank + jnp.where(key1[u] == key1[t], one, none)
        out_ref[POS + key1[t] * 4 + rank] = jnp.int32(t)

        @pl.when(row == t)
        def _():
            out_ref[OWN] = key1[t]
            out_ref[OWN + 1] = key2[t]
            out_ref[OWN + 2] = out_ref[SRC + LT + t] % 4

    for m in (2, 3):
        for k in range(m):
            for i in range(WIDTHS[m][k]):
                q = i
                if k == 1:
                    q = out_ref[OWN] * 2 + i
                if k == 2:
                    q = out_ref[OWN + 1]
                tile = out_ref[HELD + (m - 2) * LT + core * 4 + q]
                at = KEEP + (m - 2) * 16 + k * 4 + i
                out_ref[at] = structure_ref[node_ref[m, tile], k, row]
                out_ref[at + 32] = tile


def make_table(parent, tile_node, structure, row_tile):
    ids = jnp.stack([lax.axis_index("narrow"), row_tile]).astype(jnp.int32)
    return pl.pallas_call(
        table_body,
        in_specs=[pl.BlockSpec(memory_space=pltpu.SMEM)] * 4,
        out_specs=pl.BlockSpec(memory_space=pltpu.SMEM),
        out_shape=jax.ShapeDtypeStruct((128,), jnp.int32),
    )(ids, parent, tile_node, structure)


PAIRS = ((0, 2), (1, 2), (0, 3), (1, 3), (2, 3))


def pack_body(id_ref, table_ref, own_ref, other_ref, two_ref, three_ref):
    half = LT // 2
    for b, (k, m) in enumerate(PAIRS):
        out = two_ref if m == 2 else three_ref
        base = sum(WIDTHS[m][:k])
        for i in range(WIDTHS[m][k]):
            at = KEEP + (m - 2) * 16 + k * 4 + i
            tile = table_ref[at + 32]
            keep = table_ref[at] > 0
            mine = tile // half == id_ref[0]
            start = pl.multiple_of(tile % half * TILE, TILE)
            cols = slice((base + i) * TILE, (base + i + 1) * TILE)

            @pl.when(keep & mine)
            def _():
                out[:, cols] = own_ref[b, :, pl.ds(start, TILE)]

            @pl.when(keep & jnp.logical_not(mine))
            def _():
                out[:, cols] = other_ref[b, :, pl.ds(start, TILE)]

            @pl.when(jnp.logical_not(keep))
            def _():
                out[:, cols] = jnp.zeros((out.shape[0], TILE), BF)


def packed(factor, table):
    r = factor.shape[1]
    own = jnp.stack([factor[k, :, m, :] for k, m in PAIRS])
    other = lax.ppermute(own, "narrow", [(0, 1), (1, 0)])
    whole = pl.BlockSpec(memory_space=pltpu.VMEM)
    scalar = pl.BlockSpec(memory_space=pltpu.SMEM)
    return pl.pallas_call(
        pack_body,
        in_specs=[scalar, scalar, whole, whole],
        out_specs=(whole,) * 2,
        out_shape=tuple(jax.ShapeDtypeStruct((r, sum(WIDTHS[m]) * TILE), BF) for m in (2, 3)),
        compiler_params=pltpu.CompilerParams(vmem_limit_bytes=VMEM),
        cost_estimate=pl.CostEstimate(flops=1, bytes_accessed=1, transcendentals=0),
    )(lax.axis_index("narrow").astype(jnp.int32).reshape(1), table, own, other)


def sparse_body(level, shapes, mirror, table_ref, place_ref, *refs):
    row_refs, refs = refs[: len(shapes)], refs[len(shapes) :]
    out_ref, lhs, rest = refs[-3:]
    piece_refs = refs[:-3]
    r = row_refs[0].shape[-2]
    span = LT * TILE
    per = TILE // r
    q = pl.program_id(0)

    @pl.when(q == 0)
    def _():
        for ref, (_, many, at) in zip(row_refs, shapes, strict=True):
            for p in range(many):
                row, j = at[p]
                block = ref[p] if len(ref.shape) == 3 else ref[...]
                lhs[row * r : (row + 1) * r, j * span : (j + 1) * span] = block
        each = piece_refs[0].shape[0]
        for a in range(4):
            for i in range(each):
                rest[place_ref[a * each + i]] = piece_refs[a][i]

    if mirror:
        q = table_ref[OWN + level - 1]
    block = rest[:, :, pl.ds(pl.multiple_of(q * TILE, TILE), TILE)]
    total = jnp.dot(lhs[:, :span], block.reshape(span, TILE), preferred_element_type=F32)
    for j in range(1, level):
        for i in range(4 // j):
            if j == 1:
                tile = table_ref[POS + q // 2 * 4 + i]
            else:
                tile = table_ref[HELD + i * 4 + q]
            start = pl.multiple_of(j * span + tile * TILE, TILE)
            if j == 1:
                block = rest[pl.ds(tile * per, per), :, pl.ds(pl.multiple_of((4 + q % 2) * TILE, TILE), TILE)]
            else:
                block = rest[pl.ds(tile * per, per), :, 6 * TILE : 7 * TILE]
            total += jnp.dot(
                lhs[:, pl.ds(start, TILE)], block.reshape(TILE, TILE), preferred_element_type=F32
            )
    if mirror:
        out_ref[...] = total
    else:
        for p in range(level):
            value = -total[p * r : (p + 1) * r]
            if p == 1:
                value = jnp.where(table_ref[OWN] == q // 2, value, 0.0)
            if p == 2:
                value = jnp.where(table_ref[OWN + 1] == q, value, 0.0)
            out_ref[p] = value.astype(BF)


def sparse_product(level, table, place, rows, rest, mirror):
    wide = lax.axis_size("wide")
    r = rows[0][0].shape[-2]
    rows_n = 1 if mirror else level

    whole = pl.BlockSpec(memory_space=pltpu.VMEM)
    flat = [array for array, _ in rows]
    shapes = tuple((0, len(at), at) for _, at in rows)
    specs = [pl.BlockSpec(memory_space=pltpu.SMEM)] + [whole] * len(flat)
    operands = [table, place] + flat
    specs += [whole] * len(rest)
    operands += rest
    if mirror:
        shape = jax.ShapeDtypeStruct((r, TILE), F32)
        out_spec = pl.BlockSpec((r, TILE), lambda i, t: (0, 0))
    else:
        shape = jax.ShapeDtypeStruct((rows_n, r, 4 * TILE), BF)
        out_spec = pl.BlockSpec((rows_n, r, TILE), lambda i, t: (0, 0, i))
    return pl.pallas_call(
        functools.partial(sparse_body, level, shapes, mirror),
        grid_spec=pltpu.PrefetchScalarGridSpec(
            num_scalar_prefetch=1,
            grid=(1 if mirror else 4,),
            in_specs=specs,
            out_specs=out_spec,
            scratch_shapes=[
                pltpu.VMEM((rows_n * r, level * LT * TILE), BF),
                pltpu.VMEM((wide, r, rest[0].shape[-1]), BF),
            ],
        ),
        out_shape=shape,
        compiler_params=pltpu.CompilerParams(vmem_limit_bytes=VMEM),
        cost_estimate=pl.CostEstimate(flops=1, bytes_accessed=1, transcendentals=0),
    )(*operands)


def place_body(level, levels, id_ref, table_ref, own_ref, other_ref, slots_ref, full_ref):
    r = own_ref.shape[1]
    part = r // 2
    per = TILE // r
    me = id_ref[0]
    first = pl.multiple_of(me * part, part)
    for c in range(LT):
        source = table_ref[SRC + (level - 2) * LT + c]
        start = pl.multiple_of(source % 4 * TILE, TILE)

        def put(ref):
            for k in range(levels):
                full_ref[k, :, c * TILE : (c + 1) * TILE] = ref[k, :, pl.ds(start, TILE)]
                for i in range(per):
                    at = pl.multiple_of(start + i * r, r)
                    slots_ref[c * per + i, k] = ref[k, pl.ds(first, part), pl.ds(at, r)]

        @pl.when(source // 4 == me)
        def _():
            put(own_ref)

        @pl.when(source // 4 != me)
        def _():
            put(other_ref)


def place_slots(level, table, value):
    wide = lax.axis_size("wide")
    l, r, c = value.shape
    other = lax.ppermute(value, "narrow", [(0, 1), (1, 0)])
    whole = pl.BlockSpec(memory_space=pltpu.VMEM)
    scalar = pl.BlockSpec(memory_space=pltpu.SMEM)
    return pl.pallas_call(
        functools.partial(place_body, level, l),
        in_specs=[scalar, scalar, whole, whole],
        out_specs=(whole, whole),
        out_shape=(
            jax.ShapeDtypeStruct((wide, l, r // 2, r), BF),
            jax.ShapeDtypeStruct((l, r, 2 * c), BF),
        ),
        compiler_params=pltpu.CompilerParams(vmem_limit_bytes=VMEM),
        cost_estimate=pl.CostEstimate(flops=1, bytes_accessed=1, transcendentals=0),
    )(lax.axis_index("narrow").astype(jnp.int32).reshape(1), table, value, other)


def diag_body(level, id_ref, table_ref, own_ref, other_ref, diag_ref, out_ref, low_ref):
    me, row = id_ref[0], id_ref[1]
    half = LT // 2
    base = SRC + (level - 2) * LT
    for c in range(LT):
        source = table_ref[base + c]
        same = source % 4 == table_ref[base + row] % 4
        if level == 3:
            same = row == c
        cols = slice(c * TILE, (c + 1) * TILE)
        inner = jnp.where(source // 4 == me, own_ref[...], other_ref[...])
        value = jnp.where(same, diag_ref[:, cols] - inner, 0.0)
        low_ref[:, cols] = value.astype(BF)

        @pl.when(me == c // half)
        def _():
            out_ref[:, (c % half) * TILE : (c % half + 1) * TILE] = value


def diag_block(level, table, inner, diag, row_tile):
    r, span = diag.shape
    other = lax.ppermute(inner, "narrow", [(0, 1), (1, 0)])
    ids = jnp.stack([lax.axis_index("narrow"), row_tile]).astype(jnp.int32)
    whole = pl.BlockSpec(memory_space=pltpu.VMEM)
    scalar = pl.BlockSpec(memory_space=pltpu.SMEM)
    return pl.pallas_call(
        functools.partial(diag_body, level),
        in_specs=[scalar, scalar, whole, whole, whole],
        out_specs=(whole, whole),
        out_shape=(jax.ShapeDtypeStruct((r, span // 2), F32), jax.ShapeDtypeStruct((r, span), BF)),
        compiler_params=pltpu.CompilerParams(vmem_limit_bytes=VMEM),
        cost_estimate=pl.CostEstimate(flops=1, bytes_accessed=1, transcendentals=0),
    )(ids, table, inner, other, diag)


def upper_body(id_ref, first_ref, *refs):
    news, turns, diags, out_ref = refs[0:3], refs[3:5], refs[5:7], refs[7]
    for k in range(LEV - 1):
        for m in range(LEV):
            if m == k:
                value = first_ref[0] if k == 0 else diags[k - 1][...]
            elif m > k:
                value = news[m - 1][k].astype(F32)
            else:
                value = turns[k - 1][m].astype(F32)
            out_ref[k, :, m, :] = value


def lower_body(id_ref, turn_ref, diag_ref, held_ref, out_ref):
    for m in range(LEV - 1):
        out_ref[0, :, m, :] = turn_ref[m].astype(F32)
    out_ref[0, :, LEV - 1, :] = diag_ref[...]


def upper_rows(diag_inverse, news, turns, diags):
    r, c = diag_inverse.shape[1:]
    step = min(r, 32)
    shape = jax.ShapeDtypeStruct((LEV, r, LEV, c), F32)
    specs = [pl.BlockSpec((1, step, c), lambda i, n: (0, i, 0))]
    specs += [pl.BlockSpec((m, step, c), lambda i, n: (0, i, n[0])) for m in range(1, LEV)]
    specs += [pl.BlockSpec((k, step, c), lambda i, n: (0, i, n[0])) for k in range(1, LEV - 1)]
    specs += [pl.BlockSpec((step, c), lambda i, n: (i, 0)) for k in range(1, LEV - 1)]
    return pl.pallas_call(
        upper_body,
        grid_spec=pltpu.PrefetchScalarGridSpec(
            num_scalar_prefetch=1,
            grid=(r // step,),
            in_specs=specs,
            out_specs=pl.BlockSpec((LEV - 1, step, LEV, c), lambda i, n: (0, i, 0, 0)),
        ),
        out_shape=shape,
        compiler_params=pltpu.CompilerParams(vmem_limit_bytes=VMEM),
        cost_estimate=pl.CostEstimate(flops=0, bytes_accessed=40 * 2**20, transcendentals=0),
    )(lax.axis_index("narrow").astype(jnp.int32).reshape(1), diag_inverse, *news, *turns, *diags)


def lower_rows(turn, diag, held):
    r, c = diag.shape
    step = min(r, 32)
    return pl.pallas_call(
        lower_body,
        grid_spec=pltpu.PrefetchScalarGridSpec(
            num_scalar_prefetch=1,
            grid=(r // step,),
            in_specs=[
                pl.BlockSpec((LEV - 1, step, c), lambda i, n: (0, i, n[0])),
                pl.BlockSpec((step, c), lambda i, n: (i, 0)),
                pl.BlockSpec(memory_space=pl.ANY),
            ],
            out_specs=pl.BlockSpec((1, step, LEV, c), lambda i, n: (LEV - 1, i, 0, 0)),
        ),
        out_shape=jax.ShapeDtypeStruct(held.shape, F32),
        input_output_aliases={3: 0},
        compiler_params=pltpu.CompilerParams(vmem_limit_bytes=VMEM),
        cost_estimate=pl.CostEstimate(flops=0, bytes_accessed=1, transcendentals=0),
    )(lax.axis_index("narrow").astype(jnp.int32).reshape(1), turn, diag, held)


def local(factor, diag_inverse, parent, tile_node, structure):
    row_count = factor.shape[1]
    col_count = factor.shape[3]
    col_tiles = col_count // TILE
    row_id = lax.axis_index("wide")
    col_id = lax.axis_index("narrow")
    high = lax.Precision.HIGHEST
    reach = ancestors(parent)
    node_hot = (tile_node[:, :, None] == jnp.arange(M, dtype=jnp.int32)[None, None, :]).astype(
        jnp.float32
    )
    row_pos = row_id * row_count // TILE
    pos_hot = (jnp.arange(LT, dtype=jnp.int32) == row_pos).astype(jnp.float32)
    row_hot = jnp.einsum("t,ltm->lm", pos_hot, node_hot, precision=high)
    col_sel = (
        jnp.arange(LT, dtype=jnp.int32)[None, :]
        == (col_id * col_tiles + jnp.arange(col_tiles, dtype=jnp.int32))[:, None]
    ).astype(jnp.float32)
    col_hot = jnp.einsum("jt,ltm->ljm", col_sel, node_hot, precision=high)
    tile_above = jnp.einsum("ra,ba,cjb->rcj", row_hot, reach, col_hot, precision=high)
    tile_same = jnp.einsum("lm,ljm->lj", row_hot, col_hot, precision=high)
    struct_row = jnp.einsum("mlt,t->ml", structure.astype(jnp.float32), pos_hot, precision=high)
    tile_struct = jnp.einsum("cjm,mr->rcj", col_hot, struct_row, precision=high)
    above = (tile_above > 0.5).astype(jnp.int32)
    same = (tile_same > 0.5).astype(jnp.int32)

    def masked(k, m):
        return (factor[k, :, m, :] * spread(tile_struct[k, m])[None, :].astype(BF))[None]

    place = positions(False)

    def panel_of(level):
        return jnp.concatenate([masked(k, level) for k in range(level)], axis=0)

    wide = lax.axis_size("wide")
    whole_place = jnp.arange(wide, dtype=jnp.int32)
    compact = lax.axis_size("narrow") == 2 and row_count % 128 == 0 and TILE % row_count == 0
    first = along_z(panel_of(1), None)
    if compact:
        table = make_table(parent, tile_node, structure, row_pos)
        shards = packed(factor, table)
        wide_diag = {m: narrow_all(diag_inverse[m], 1) for m in (2, 3)}
    else:
        panels = {m: lax.all_gather(panel_of(m), "wide", axis=0) for m in (2, 3)}
    one = along_xy(first, None)
    if compact:
        second = along_line(after(shards[0], one[0]), None)
    one = along_both(one, (one[2],) if compact else None)

    held = {}
    rows = {0: [(narrow_all(diag_inverse[0].astype(BF), 1), ((0, 0),))]}
    news, turns, diags = [], [], []
    rest = []
    for level in range(1, LEV):
        packed_here = compact and level > 1
        if packed_here:
            known = [part for k in range(level) for part in rows[k]] + [held[m] for m in range(1, level)]
            if level == 2:
                held_line = lax.optimization_barrier(tuple(third[0] + third[1]) + (diags[0],))
                depth = len(third[0])
                ahead = along_xy(line_pieces(held_line[:depth], held_line[depth:-1], third[2]), None)
            value = sparse_product(level, table, place, known, rest, False)
            slots, full = place_slots(level, table, value)
        else:
            if level == 1:
                groups = [((0,), place, one)]
                known = [[rows[0][0][0]]]
                if compact:
                    known[0][0] = after(known[0][0], *second[0][1:], *second[1][1:])
            else:
                groups = [(tuple(range(level)), whole_place, [panels[level]])]
                known = []
                for k in range(level):
                    by_level = {}
                    for array, at in rows[k] + [held[m] for m in range(1, level)]:
                        for p, (row, j) in enumerate(at):
                            if row == k:
                                by_level[j] = array[p] if array.ndim == 3 else array
                    known.append([by_level[j] for j in range(level)])
            value = product(known, groups, above[:level, level])
            if compact:
                held_line = lax.optimization_barrier(tuple(second[0] + second[1]) + (value,))
                depth = len(second[0])
                ahead = along_xy(line_pieces(held_line[:depth], held_line[depth:-1], second[2]), None)
                third = along_line(after(shards[1], ahead[0]), None)
            slots, full = make_slots(value)
        news.append(full)
        held[level] = (full, tuple((k, level) for k in range(level)))
        if level == LEV - 1:
            out = upper_rows(diag_inverse, news, turns, diags)
        got = lax.all_to_all(slots, "wide", split_axis=0, concat_axis=0, tiled=True)
        if level == LEV - 1:
            got = after(got, out)
        now = rest
        if compact and level < LEV - 1:
            if level == 1:
                rest = along_both(ahead, (got, ahead[2]) + tuple(third[0][1:] + third[1][1:]))
                got = after(got, ahead[1], ahead[2])
            else:
                rest = along_both(ahead, (slots, ahead[2]))
                got = after(got, ahead[1], ahead[2])
        turn = mirrored(got, full)
        turns.append(turn)
        rows[level] = [(turn, tuple((level, j) for j in range(level)))]
        if packed_here:
            here = [(turn, tuple((0, j) for j in range(level)))]
            inner = sparse_product(level, table, place, here, now, True)
            done, whole_low = diag_block(level, table, inner, wide_diag[level], row_pos)
        else:
            known = [[turn[k] for k in range(level)]]
            done, low = product(known, groups, same[level : level + 1], (diag_inverse, level))
            whole_low = narrow_all(low, 1) if level < LEV - 1 else None
        diags.append(done)
        if level < LEV - 1:
            rows[level].append((whole_low, ((level, level),)))
    return lower_rows(turns[-1], diags[-1], out)


def solution(mesh):
    return jax.shard_map(
        local,
        mesh=mesh,
        in_specs=(P(None, "wide", None, "narrow"), P(None, "wide", "narrow"), P(), P(), P()),
        out_specs=P(None, "wide", None, "narrow"),
        check_vma=False,
    )
```

```python
import functools

import jax
import jax.numpy as jnp
from jax import lax
from jax.experimental import pallas as pl
from jax.experimental.pallas import tpu as pltpu
from jax.sharding import PartitionSpec as P

LEV = 4
TILE = 256
LT = 8
M = 15
BF = jnp.bfloat16
F32 = jnp.float32
VMEM = 56 * 1024 * 1024


def ancestors(parent):
    node_ids = jnp.arange(M, dtype=jnp.int32)
    step_mat = (parent[:, None] == node_ids[None, :]).astype(jnp.float32)
    power_mat = step_mat
    reach = step_mat
    for hop_count in range(LEV - 2):
        power_mat = jnp.dot(power_mat, step_mat, precision=lax.Precision.HIGHEST)
        reach = reach + power_mat
    return reach


def spread(mask_tile):
    return jnp.repeat(mask_tile, TILE, axis=-1)


def after(value, *others):
    return lax.optimization_barrier((value,) + others)[0]


def narrow_all(x, axis):
    size = lax.axis_size("narrow")
    mine = lax.axis_index("narrow")
    if size == 2:
        other = lax.ppermute(x, "narrow", [(0, 1), (1, 0)])
        first = mine == 0
        return jnp.concatenate([jnp.where(first, x, other), jnp.where(first, other, x)], axis=axis)
    shape = list(x.shape)
    width = shape[axis]
    shape[axis] = width * size
    out = jnp.zeros(shape, x.dtype)
    for hop in range(size):
        got = x if hop == 0 else lax.ppermute(x, "narrow", [(i, (i + hop) % size) for i in range(size)])
        out = lax.dynamic_update_slice_in_dim(out, got, (mine - hop) % size * width, axis)
    return out


def swap(value, turn):
    wide = lax.axis_size("wide")
    narrow = lax.axis_size("narrow")
    pairs = []
    for i in range(wide):
        for j in range(narrow):
            pairs.append((i * narrow + j, (i ^ (1 if (j + turn) % 2 == 0 else 2)) * narrow + j))
    return lax.ppermute(value, ("wide", "narrow"), pairs)


def shifts(value):
    wide = lax.axis_size("wide")
    return [value] + [
        lax.ppermute(value, "wide", [(i, (i + 4 * hop) % wide) for i in range(wide)])
        for hop in range(1, wide // 4)
    ]


def positions(z_last):
    wide = lax.axis_size("wide")
    depth = wide // 4
    row_id = lax.axis_index("wide")
    odd = lax.axis_index("narrow") % 2
    z = (row_id // 4 - jnp.arange(depth, dtype=jnp.int32)) % depth
    flips = jnp.stack([0 * odd, 1 + odd, 2 - odd, 3 + 0 * odd])
    near = (row_id % 4) ^ flips
    if z_last:
        return (z[:, None] * 4 + near[None, :]).reshape(-1).astype(jnp.int32)
    return (z[None, :] * 4 + near[:, None]).reshape(-1).astype(jnp.int32)


def along_z(x, gate):
    return shifts(x if gate is None else after(x, gate))


def along_line(x, gate):
    wide = lax.axis_size("wide")
    depth = wide // 4
    z = lax.axis_index("wide") // 4
    up = down = x if gate is None else after(x, gate)
    ups, downs = [up], [down]
    for hop in range(1, depth):
        up = lax.ppermute(up, "wide", [(i, i + 4) for i in range(4 * (hop - 1), wide - 4)])
        down = lax.ppermute(down, "wide", [(i, i - 4) for i in range(4, wide - 4 * (hop - 1))])
        ups.append(up)
        downs.append(down)
    return ups, downs, [z >= hop for hop in range(depth)]


def line_pieces(ups, downs, below):
    depth = len(ups)
    return [ups[0]] + [jnp.where(below[k], ups[k], downs[depth - k]) for k in range(1, depth)]


def along_xy(pieces, gate):
    if gate is not None:
        held = lax.optimization_barrier(tuple(pieces) + (gate,))
        pieces = held[:-1]
    line = jnp.stack(pieces)
    return [line, swap(line, 0), swap(line, 1)]


def along_both(arrays, gate):
    near = arrays[1]
    return arrays + [swap(near if gate is None else after(near, *gate), 1)]


def product_body(plan, rows_n, steps_n, finish, *refs):
    place_ref, mask_ref = refs[0], refs[1]
    refs = refs[2:]
    row_refs = [refs[q * steps_n : (q + 1) * steps_n] for q in range(rows_n)]
    refs = refs[rows_n * steps_n :]
    count = sum(arrays for _, arrays, _ in plan)
    piece_refs, refs = refs[:count], refs[count:]
    if finish:
        diag_ref, out_ref, low_ref, lhs = refs
    else:
        out_ref, lhs = refs
    r = row_refs[0][0].shape[0]
    width = piece_refs[0].shape[-1]

    @pl.when(pl.program_id(0) == 0)
    def _():
        at = 0
        for g, (levels, arrays, each) in enumerate(plan):
            for i in range(arrays * each):
                start = pl.multiple_of(place_ref[g, i] * r, r)
                for j in levels:
                    for q in range(rows_n):
                        lhs[q * r : (q + 1) * r, at : at + r] = row_refs[q][j][:, pl.ds(start, r)]
                    at += r

    total = None
    at, base = 0, 0
    for levels, arrays, each in plan:
        depth = each * len(levels) * r
        for a in range(arrays):
            part = jnp.dot(
                lhs[:, at : at + depth],
                piece_refs[base + a][...].reshape(depth, width),
                preferred_element_type=F32,
            )
            total = part if total is None else total + part
            at += depth
        base += arrays
    here = pl.program_id(0)
    for q in range(rows_n):
        for t in range(width // TILE):
            keep = mask_ref[q, here * (width // TILE) + t] > 0
            cols = slice(t * TILE, (t + 1) * TILE)
            value = total[q * r : (q + 1) * r, cols]
            if finish:
                value = diag_ref[0, :, cols] - value
            else:
                value = -value
            value = jnp.where(keep, value, 0.0)
            if finish:
                out_ref[:, cols] = value
                low_ref[:, cols] = value.astype(BF)
            else:
                out_ref[q, :, cols] = value.astype(BF)


def product(rows, groups, mask, diag=None, shift=0):
    r = rows[0][0].shape[0]
    c = groups[0][2][0].shape[-1]
    rows_n, steps_n = len(rows), len(rows[0])
    if r % 128:
        total = 0.0
        for levels, place, arrays in groups:
            at = 0
            for array in arrays:
                each = array.shape[0]
                here = place[at : at + each]
                lhs = jnp.concatenate(
                    [
                        jnp.stack(
                            [jnp.take(row[j].reshape(r, -1, r), here, axis=1) for j in levels], axis=2
                        ).reshape(r, -1)
                        for row in rows
                    ],
                    axis=0,
                )
                total += jnp.dot(lhs, array.reshape(-1, c), preferred_element_type=F32)
                at += each
        total = total.reshape(rows_n, r, c)
        keep = jnp.repeat(mask, TILE, axis=1)[:, None, :] > 0
        if diag is None:
            return jnp.where(keep, -total, 0.0).astype(BF)
        level = diag[1]
        value = jnp.where(keep[0], diag[0][level, :, shift : shift + c] - total[0], 0.0)
        return value, value.astype(BF)
    width = TILE
    plan = tuple((tuple(levels), len(arrays), arrays[0].shape[0]) for levels, _, arrays in groups)
    place = jnp.stack([p for _, p, _ in groups])
    whole = pl.BlockSpec(memory_space=pltpu.VMEM)
    scalar = pl.BlockSpec(memory_space=pltpu.SMEM)
    pieces = [a for _, _, arrays in groups for a in arrays]
    piece_specs = [pl.BlockSpec(a.shape[:3] + (width,), lambda i: (0, 0, 0, i)) for a in pieces]
    flat = [x for row in rows for x in row]
    operands = [place, mask] + flat + pieces
    specs = [scalar, scalar] + [whole] * len(flat) + piece_specs
    if diag is None:
        outs = jax.ShapeDtypeStruct((rows_n, r, c), BF)
        out_specs = pl.BlockSpec((rows_n, r, width), lambda i: (0, 0, i))
    else:
        level = diag[1]
        skip = shift // width
        operands.append(diag[0])
        specs.append(pl.BlockSpec((1, r, width), lambda i: (level, 0, skip + i)))
        outs = (jax.ShapeDtypeStruct((r, c), F32), jax.ShapeDtypeStruct((r, c), BF))
        out_specs = (pl.BlockSpec((r, width), lambda i: (0, i)),) * 2
    deep = sum(len(levels) * arrays * each for levels, arrays, each in plan) * r
    return pl.pallas_call(
        functools.partial(product_body, plan, rows_n, steps_n, diag is not None),
        grid=(c // width,),
        in_specs=specs,
        out_specs=out_specs,
        out_shape=outs,
        scratch_shapes=[pltpu.VMEM((rows_n * r, deep), BF)],
        compiler_params=pltpu.CompilerParams(vmem_limit_bytes=VMEM),
        cost_estimate=pl.CostEstimate(
            flops=1, bytes_accessed=1, transcendentals=0
        ),
    )(*operands)


def slots_body(levels, wide, id_ref, own_ref, other_ref, slots_ref, full_ref):
    r, c = own_ref.shape[1:]
    part = r // 2
    half = wide // 2
    for n in range(2):

        @pl.when(id_ref[0] == n)
        def _():
            for h in range(2):
                ref = own_ref if h == n else other_ref
                for k in range(levels):
                    full_ref[k, :, h * c : (h + 1) * c] = ref[k]
                    for i in range(half):
                        slots_ref[h * half + i, k] = ref[k, n * part : (n + 1) * part, i * r : (i + 1) * r]


def make_slots(value):
    wide = lax.axis_size("wide")
    narrow = lax.axis_size("narrow")
    l, r, c = value.shape
    if narrow != 2 or r % 128:
        full = narrow_all(value, 2)
        part = r // narrow
        mine = lax.dynamic_slice_in_dim(full, lax.axis_index("narrow") * part, part, 1)
        return mine.reshape(l, part, wide, r).transpose(2, 0, 1, 3), full
    other = lax.ppermute(value, "narrow", [(0, 1), (1, 0)])
    whole = pl.BlockSpec(memory_space=pltpu.VMEM)
    return pl.pallas_call(
        functools.partial(slots_body, l, wide),
        in_specs=[pl.BlockSpec(memory_space=pltpu.SMEM), whole, whole],
        out_specs=(whole, whole),
        out_shape=(
            jax.ShapeDtypeStruct((wide, l, r // 2, r), BF),
            jax.ShapeDtypeStruct((l, r, 2 * c), BF),
        ),
        compiler_params=pltpu.CompilerParams(vmem_limit_bytes=VMEM),
        cost_estimate=pl.CostEstimate(flops=1, bytes_accessed=1, transcendentals=0),
    )(lax.axis_index("narrow").astype(jnp.int32).reshape(1), value, other)


def turn_body(levels, wide, id_ref, own_ref, other_ref, out_ref):
    r = out_ref.shape[1]
    for n in range(2):

        @pl.when(id_ref[0] == n)
        def _():
            first, second = (own_ref, other_ref) if n == 0 else (other_ref, own_ref)
            for k in range(levels):
                for w in range(wide):
                    block = jnp.concatenate([first[w, k], second[w, k]], axis=0)
                    out_ref[k, :, w * r : (w + 1) * r] = block.T


def mirrored(got, full):
    wide = lax.axis_size("wide")
    narrow = lax.axis_size("narrow")
    l, r, cols = full.shape
    if narrow != 2 or r % 128:
        return narrow_all(got, 2).transpose(1, 3, 0, 2).reshape(l, r, cols)
    other = lax.ppermute(got, "narrow", [(0, 1), (1, 0)])
    whole = pl.BlockSpec(memory_space=pltpu.VMEM)
    return pl.pallas_call(
        functools.partial(turn_body, l, wide),
        in_specs=[pl.BlockSpec(memory_space=pltpu.SMEM), whole, whole],
        out_specs=whole,
        out_shape=jax.ShapeDtypeStruct((l, r, cols), BF),
        compiler_params=pltpu.CompilerParams(vmem_limit_bytes=VMEM),
        cost_estimate=pl.CostEstimate(flops=1, bytes_accessed=1, transcendentals=0),
    )(lax.axis_index("narrow").astype(jnp.int32).reshape(1), got, other)


SRC, POS, HELD, OWN, KEEP = 0, 16, 24, 40, 48
WIDTHS = {2: (4, 2), 3: (4, 2, 1)}


def table_body(id_ref, parent_ref, node_ref, structure_ref, out_ref):
    core, row = id_ref[0], id_ref[1]
    for i in range(out_ref.shape[0]):
        out_ref[i] = jnp.int32(0)
    one, none = jnp.int32(1), jnp.int32(0)
    nodes = [[node_ref[k, t] for t in range(LT)] for k in range(LEV)]
    above = [[parent_ref[nodes[k][t]] for t in range(LT)] for k in range(LEV)]
    left = nodes[1][0]
    key1 = [jnp.where(nodes[1][t] == left, none, one) for t in range(LT)]

    def second(k, t):
        found = none
        for u in range(LT):
            less = (above[k][u] == above[k][t]) & (nodes[k][u] < nodes[k][t])
            found = jnp.where(less, one, found)
        return found

    key2 = [jnp.where(above[2][t] == left, none, 2 * one) + second(2, t) for t in range(LT)]
    for t in range(LT):
        again = none
        for u in range(t):
            again = jnp.where(nodes[2][u] == nodes[2][t], one, again)
        place = again * 4 + key2[t]
        out_ref[SRC + t] = place
        out_ref[HELD + place] = jnp.int32(t)
        upper = none
        for u in range(LT):
            upper = jnp.where(nodes[2][u] == above[3][t], key2[u], upper)
        place = second(3, t) * 4 + upper
        out_ref[SRC + LT + t] = place
        out_ref[HELD + LT + place] = jnp.int32(t)
        rank = none
        for u in range(t):
            rank = rank + jnp.where(key1[u] == key1[t], one, none)
        out_ref[POS + key1[t] * 4 + rank] = jnp.int32(t)

        @pl.when(row == t)
        def _():
            out_ref[OWN] = key1[t]
            out_ref[OWN + 1] = key2[t]
            out_ref[OWN + 2] = out_ref[SRC + LT + t] % 4

    for m in (2, 3):
        for k in range(m):
            for i in range(WIDTHS[m][k]):
                q = i
                if k == 1:
                    q = out_ref[OWN] * 2 + i
                if k == 2:
                    q = out_ref[OWN + 1]
                tile = out_ref[HELD + (m - 2) * LT + core * 4 + q]
                at = KEEP + (m - 2) * 16 + k * 4 + i
                out_ref[at] = structure_ref[node_ref[m, tile], k, row]
                out_ref[at + 32] = tile


def make_table(parent, tile_node, structure, row_tile):
    ids = jnp.stack([lax.axis_index("narrow"), row_tile]).astype(jnp.int32)
    return pl.pallas_call(
        table_body,
        in_specs=[pl.BlockSpec(memory_space=pltpu.SMEM)] * 4,
        out_specs=pl.BlockSpec(memory_space=pltpu.SMEM),
        out_shape=jax.ShapeDtypeStruct((128,), jnp.int32),
    )(ids, parent, tile_node, structure)


PAIRS = ((0, 2), (1, 2), (0, 3), (1, 3), (2, 3))


def pack_body(id_ref, table_ref, own_ref, other_ref, two_ref, three_ref):
    half = LT // 2
    for b, (k, m) in enumerate(PAIRS):
        out = two_ref if m == 2 else three_ref
        base = sum(WIDTHS[m][:k])
        for i in range(WIDTHS[m][k]):
            at = KEEP + (m - 2) * 16 + k * 4 + i
            tile = table_ref[at + 32]
            keep = table_ref[at] > 0
            mine = tile // half == id_ref[0]
            start = pl.multiple_of(tile % half * TILE, TILE)
            cols = slice((base + i) * TILE, (base + i + 1) * TILE)

            @pl.when(keep & mine)
            def _():
                out[:, cols] = own_ref[b, :, pl.ds(start, TILE)]

            @pl.when(keep & jnp.logical_not(mine))
            def _():
                out[:, cols] = other_ref[b, :, pl.ds(start, TILE)]

            @pl.when(jnp.logical_not(keep))
            def _():
                out[:, cols] = jnp.zeros((out.shape[0], TILE), BF)


def packed(factor, table):
    r = factor.shape[1]
    own = jnp.stack([factor[k, :, m, :] for k, m in PAIRS])
    other = lax.ppermute(own, "narrow", [(0, 1), (1, 0)])
    whole = pl.BlockSpec(memory_space=pltpu.VMEM)
    scalar = pl.BlockSpec(memory_space=pltpu.SMEM)
    return pl.pallas_call(
        pack_body,
        in_specs=[scalar, scalar, whole, whole],
        out_specs=(whole,) * 2,
        out_shape=tuple(jax.ShapeDtypeStruct((r, sum(WIDTHS[m]) * TILE), BF) for m in (2, 3)),
        compiler_params=pltpu.CompilerParams(vmem_limit_bytes=VMEM),
        cost_estimate=pl.CostEstimate(flops=1, bytes_accessed=1, transcendentals=0),
    )(lax.axis_index("narrow").astype(jnp.int32).reshape(1), table, own, other)


def sparse_body(level, shapes, mirror, table_ref, place_ref, *refs):
    row_refs, refs = refs[: len(shapes)], refs[len(shapes) :]
    out_ref, lhs, rest = refs[-3:]
    piece_refs = refs[:-3]
    r = row_refs[0].shape[-2]
    span = LT * TILE
    per = TILE // r
    q = pl.program_id(0)

    @pl.when(q == 0)
    def _():
        for ref, (_, many, at) in zip(row_refs, shapes, strict=True):
            for p in range(many):
                row, j = at[p]
                block = ref[p] if len(ref.shape) == 3 else ref[...]
                lhs[row * r : (row + 1) * r, j * span : (j + 1) * span] = block
        each = piece_refs[0].shape[0]
        for a in range(4):
            for i in range(each):
                rest[place_ref[a * each + i]] = piece_refs[a][i]

    if mirror:
        q = table_ref[OWN + level - 1]
    block = rest[:, :, pl.ds(pl.multiple_of(q * TILE, TILE), TILE)]
    total = jnp.dot(lhs[:, :span], block.reshape(span, TILE), preferred_element_type=F32)
    for j in range(1, level):
        for i in range(4 // j):
            if j == 1:
                tile = table_ref[POS + q // 2 * 4 + i]
            else:
                tile = table_ref[HELD + i * 4 + q]
            start = pl.multiple_of(j * span + tile * TILE, TILE)
            if j == 1:
                block = rest[pl.ds(tile * per, per), :, pl.ds(pl.multiple_of((4 + q % 2) * TILE, TILE), TILE)]
            else:
                block = rest[pl.ds(tile * per, per), :, 6 * TILE : 7 * TILE]
            total += jnp.dot(
                lhs[:, pl.ds(start, TILE)], block.reshape(TILE, TILE), preferred_element_type=F32
            )
    if mirror:
        out_ref[...] = total
    else:
        for p in range(level):
            value = -total[p * r : (p + 1) * r]
            if p == 1:
                value = jnp.where(table_ref[OWN] == q // 2, value, 0.0)
            if p == 2:
                value = jnp.where(table_ref[OWN + 1] == q, value, 0.0)
            out_ref[p] = value.astype(BF)


def sparse_product(level, table, place, rows, rest, mirror):
    wide = lax.axis_size("wide")
    r = rows[0][0].shape[-2]
    rows_n = 1 if mirror else level

    whole = pl.BlockSpec(memory_space=pltpu.VMEM)
    flat = [array for array, _ in rows]
    shapes = tuple((0, len(at), at) for _, at in rows)
    specs = [pl.BlockSpec(memory_space=pltpu.SMEM)] + [whole] * len(flat)
    operands = [table, place] + flat
    specs += [whole] * len(rest)
    operands += rest
    if mirror:
        shape = jax.ShapeDtypeStruct((r, TILE), F32)
        out_spec = pl.BlockSpec((r, TILE), lambda i, t: (0, 0))
    else:
        shape = jax.ShapeDtypeStruct((rows_n, r, 4 * TILE), BF)
        out_spec = pl.BlockSpec((rows_n, r, TILE), lambda i, t: (0, 0, i))
    return pl.pallas_call(
        functools.partial(sparse_body, level, shapes, mirror),
        grid_spec=pltpu.PrefetchScalarGridSpec(
            num_scalar_prefetch=1,
            grid=(1 if mirror else 4,),
            in_specs=specs,
            out_specs=out_spec,
            scratch_shapes=[
                pltpu.VMEM((rows_n * r, level * LT * TILE), BF),
                pltpu.VMEM((wide, r, rest[0].shape[-1]), BF),
            ],
        ),
        out_shape=shape,
        compiler_params=pltpu.CompilerParams(vmem_limit_bytes=VMEM),
        cost_estimate=pl.CostEstimate(flops=1, bytes_accessed=1, transcendentals=0),
    )(*operands)


def place_body(level, levels, id_ref, table_ref, own_ref, other_ref, slots_ref, full_ref):
    r = own_ref.shape[1]
    part = r // 2
    per = TILE // r
    me = id_ref[0]
    first = pl.multiple_of(me * part, part)
    for c in range(LT):
        source = table_ref[SRC + (level - 2) * LT + c]
        start = pl.multiple_of(source % 4 * TILE, TILE)

        def put(ref):
            for k in range(levels):
                full_ref[k, :, c * TILE : (c + 1) * TILE] = ref[k, :, pl.ds(start, TILE)]
                for i in range(per):
                    at = pl.multiple_of(start + i * r, r)
                    slots_ref[c * per + i, k] = ref[k, pl.ds(first, part), pl.ds(at, r)]

        @pl.when(source // 4 == me)
        def _():
            put(own_ref)

        @pl.when(source // 4 != me)
        def _():
            put(other_ref)


def place_slots(level, table, value):
    wide = lax.axis_size("wide")
    l, r, c = value.shape
    other = lax.ppermute(value, "narrow", [(0, 1), (1, 0)])
    whole = pl.BlockSpec(memory_space=pltpu.VMEM)
    scalar = pl.BlockSpec(memory_space=pltpu.SMEM)
    return pl.pallas_call(
        functools.partial(place_body, level, l),
        in_specs=[scalar, scalar, whole, whole],
        out_specs=(whole, whole),
        out_shape=(
            jax.ShapeDtypeStruct((wide, l, r // 2, r), BF),
            jax.ShapeDtypeStruct((l, r, 2 * c), BF),
        ),
        compiler_params=pltpu.CompilerParams(vmem_limit_bytes=VMEM),
        cost_estimate=pl.CostEstimate(flops=1, bytes_accessed=1, transcendentals=0),
    )(lax.axis_index("narrow").astype(jnp.int32).reshape(1), table, value, other)


def diag_body(level, id_ref, table_ref, own_ref, other_ref, diag_ref, out_ref, low_ref):
    me, row = id_ref[0], id_ref[1]
    half = LT // 2
    base = SRC + (level - 2) * LT
    for c in range(LT):
        source = table_ref[base + c]
        same = source % 4 == table_ref[base + row] % 4
        if level == 3:
            same = row == c
        cols = slice(c * TILE, (c + 1) * TILE)
        inner = jnp.where(source // 4 == me, own_ref[...], other_ref[...])
        value = jnp.where(same, diag_ref[:, cols] - inner, 0.0)
        low_ref[:, cols] = value.astype(BF)

        @pl.when(me == c // half)
        def _():
            out_ref[:, (c % half) * TILE : (c % half + 1) * TILE] = value


def diag_block(level, table, inner, diag, row_tile):
    r, span = diag.shape
    other = lax.ppermute(inner, "narrow", [(0, 1), (1, 0)])
    ids = jnp.stack([lax.axis_index("narrow"), row_tile]).astype(jnp.int32)
    whole = pl.BlockSpec(memory_space=pltpu.VMEM)
    scalar = pl.BlockSpec(memory_space=pltpu.SMEM)
    return pl.pallas_call(
        functools.partial(diag_body, level),
        in_specs=[scalar, scalar, whole, whole, whole],
        out_specs=(whole, whole),
        out_shape=(jax.ShapeDtypeStruct((r, span // 2), F32), jax.ShapeDtypeStruct((r, span), BF)),
        compiler_params=pltpu.CompilerParams(vmem_limit_bytes=VMEM),
        cost_estimate=pl.CostEstimate(flops=1, bytes_accessed=1, transcendentals=0),
    )(ids, table, inner, other, diag)


def upper_body(id_ref, first_ref, *refs):
    news, turns, diags, out_ref = refs[0:3], refs[3:5], refs[5:7], refs[7]
    for k in range(LEV - 1):
        for m in range(LEV):
            if m == k:
                value = first_ref[0] if k == 0 else diags[k - 1][...]
            elif m > k:
                value = news[m - 1][k].astype(F32)
            else:
                value = turns[k - 1][m].astype(F32)
            out_ref[k, :, m, :] = value


def lower_body(id_ref, turn_ref, diag_ref, held_ref, out_ref):
    for m in range(LEV - 1):
        out_ref[0, :, m, :] = turn_ref[m].astype(F32)
    out_ref[0, :, LEV - 1, :] = diag_ref[...]


def upper_rows(diag_inverse, news, turns, diags):
    r, c = diag_inverse.shape[1:]
    step = min(r, 32)
    shape = jax.ShapeDtypeStruct((LEV, r, LEV, c), F32)
    specs = [pl.BlockSpec((1, step, c), lambda i, n: (0, i, 0))]
    specs += [pl.BlockSpec((m, step, c), lambda i, n: (0, i, n[0])) for m in range(1, LEV)]
    specs += [pl.BlockSpec((k, step, c), lambda i, n: (0, i, n[0])) for k in range(1, LEV - 1)]
    specs += [pl.BlockSpec((step, c), lambda i, n: (i, 0)) for k in range(1, LEV - 1)]
    return pl.pallas_call(
        upper_body,
        grid_spec=pltpu.PrefetchScalarGridSpec(
            num_scalar_prefetch=1,
            grid=(r // step,),
            in_specs=specs,
            out_specs=pl.BlockSpec((LEV - 1, step, LEV, c), lambda i, n: (0, i, 0, 0)),
        ),
        out_shape=shape,
        compiler_params=pltpu.CompilerParams(vmem_limit_bytes=VMEM),
        cost_estimate=pl.CostEstimate(flops=0, bytes_accessed=40 * 2**20, transcendentals=0),
    )(lax.axis_index("narrow").astype(jnp.int32).reshape(1), diag_inverse, *news, *turns, *diags)


def lower_rows(turn, diag, held):
    r, c = diag.shape
    step = min(r, 32)
    return pl.pallas_call(
        lower_body,
        grid_spec=pltpu.PrefetchScalarGridSpec(
            num_scalar_prefetch=1,
            grid=(r // step,),
            in_specs=[
                pl.BlockSpec((LEV - 1, step, c), lambda i, n: (0, i, n[0])),
                pl.BlockSpec((step, c), lambda i, n: (i, 0)),
                pl.BlockSpec(memory_space=pl.ANY),
            ],
            out_specs=pl.BlockSpec((1, step, LEV, c), lambda i, n: (LEV - 1, i, 0, 0)),
        ),
        out_shape=jax.ShapeDtypeStruct(held.shape, F32),
        input_output_aliases={3: 0},
        compiler_params=pltpu.CompilerParams(vmem_limit_bytes=VMEM),
        cost_estimate=pl.CostEstimate(flops=0, bytes_accessed=1, transcendentals=0),
    )(lax.axis_index("narrow").astype(jnp.int32).reshape(1), turn, diag, held)


def local(factor, diag_inverse, parent, tile_node, structure):
    row_count = factor.shape[1]
    col_count = factor.shape[3]
    col_tiles = col_count // TILE
    row_id = lax.axis_index("wide")
    col_id = lax.axis_index("narrow")
    high = lax.Precision.HIGHEST
    reach = ancestors(parent)
    node_hot = (tile_node[:, :, None] == jnp.arange(M, dtype=jnp.int32)[None, None, :]).astype(
        jnp.float32
    )
    row_pos = row_id * row_count // TILE
    pos_hot = (jnp.arange(LT, dtype=jnp.int32) == row_pos).astype(jnp.float32)
    row_hot = jnp.einsum("t,ltm->lm", pos_hot, node_hot, precision=high)
    col_sel = (
        jnp.arange(LT, dtype=jnp.int32)[None, :]
        == (col_id * col_tiles + jnp.arange(col_tiles, dtype=jnp.int32))[:, None]
    ).astype(jnp.float32)
    col_hot = jnp.einsum("jt,ltm->ljm", col_sel, node_hot, precision=high)
    tile_above = jnp.einsum("ra,ba,cjb->rcj", row_hot, reach, col_hot, precision=high)
    tile_same = jnp.einsum("lm,ljm->lj", row_hot, col_hot, precision=high)
    struct_row = jnp.einsum("mlt,t->ml", structure.astype(jnp.float32), pos_hot, precision=high)
    tile_struct = jnp.einsum("cjm,mr->rcj", col_hot, struct_row, precision=high)
    above = (tile_above > 0.5).astype(jnp.int32)
    same = (tile_same > 0.5).astype(jnp.int32)

    def masked(k, m):
        return (factor[k, :, m, :] * spread(tile_struct[k, m])[None, :].astype(BF))[None]

    place = positions(False)

    def panel_of(level):
        return jnp.concatenate([masked(k, level) for k in range(level)], axis=0)

    wide = lax.axis_size("wide")
    whole_place = jnp.arange(wide, dtype=jnp.int32)
    compact = lax.axis_size("narrow") == 2 and row_count % 128 == 0 and TILE % row_count == 0
    first = along_z(panel_of(1), None)
    if compact:
        table = make_table(parent, tile_node, structure, row_pos)
        shards = packed(factor, table)
        wide_diag = {m: narrow_all(diag_inverse[m], 1) for m in (2, 3)}
    else:
        panels = {m: lax.all_gather(panel_of(m), "wide", axis=0) for m in (2, 3)}
    one = along_xy(first, None)
    if compact:
        second = along_line(after(shards[0], one[0]), None)
    one = along_both(one, (one[2],) if compact else None)

    held = {}
    rows = {0: [(narrow_all(diag_inverse[0].astype(BF), 1), ((0, 0),))]}
    news, turns, diags = [], [], []
    rest = []
    for level in range(1, LEV):
        packed_here = compact and level > 1
        if packed_here:
            known = [part for k in range(level) for part in rows[k]] + [held[m] for m in range(1, level)]
            if level == 2:
                held_line = lax.optimization_barrier(tuple(third[0] + third[1]) + (diags[0],))
                depth = len(third[0])
                ahead = along_xy(line_pieces(held_line[:depth], held_line[depth:-1], third[2]), None)
            value = sparse_product(level, table, place, known, rest, False)
            slots, full = place_slots(level, table, value)
        else:
            if level == 1:
                groups = [((0,), place, one)]
                known = [[rows[0][0][0]]]
                if compact:
                    known[0][0] = after(known[0][0], *second[0][1:], *second[1][1:])
            else:
                groups = [(tuple(range(level)), whole_place, [panels[level]])]
                known = []
                for k in range(level):
                    by_level = {}
                    for array, at in rows[k] + [held[m] for m in range(1, level)]:
                        for p, (row, j) in enumerate(at):
                            if row == k:
                                by_level[j] = array[p] if array.ndim == 3 else array
                    known.append([by_level[j] for j in range(level)])
            value = product(known, groups, above[:level, level])
            if compact:
                held_line = lax.optimization_barrier(tuple(second[0] + second[1]) + (one[-1],))
                depth = len(second[0])
                ahead = along_xy(line_pieces(held_line[:depth], held_line[depth:-1], second[2]), None)
                third = along_line(after(shards[1], ahead[0]), None)
            slots, full = make_slots(value)
        news.append(full)
        held[level] = (full, tuple((k, level) for k in range(level)))
        if level == LEV - 1:
            out = upper_rows(diag_inverse, news, turns, diags)
        got = lax.all_to_all(slots, "wide", split_axis=0, concat_axis=0, tiled=True)
        if level == LEV - 1:
            got = after(got, out)
        now = rest
        if compact and level < LEV - 1:
            if level == 1:
                rest = along_both(ahead, (got, ahead[2]) + tuple(third[0][1:] + third[1][1:]))
                got = after(got, ahead[1], ahead[2])
            else:
                rest = along_both(ahead, (slots, ahead[2]))
                got = after(got, ahead[1], ahead[2])
        turn = mirrored(got, full)
        turns.append(turn)
        rows[level] = [(turn, tuple((level, j) for j in range(level)))]
        if packed_here:
            here = [(turn, tuple((0, j) for j in range(level)))]
            inner = sparse_product(level, table, place, here, now, True)
            done, whole_low = diag_block(level, table, inner, wide_diag[level], row_pos)
        else:
            known = [[turn[k] for k in range(level)]]
            done, low = product(known, groups, same[level : level + 1], (diag_inverse, level))
            whole_low = narrow_all(low, 1) if level < LEV - 1 else None
        diags.append(done)
        if level < LEV - 1:
            rows[level].append((whole_low, ((level, level),)))
    return lower_rows(turns[-1], diags[-1], out)


def solution(mesh):
    return jax.shard_map(
        local,
        mesh=mesh,
        in_specs=(P(None, "wide", None, "narrow"), P(None, "wide", "narrow"), P(), P(), P()),
        out_specs=P(None, "wide", None, "narrow"),
        check_vma=False,
    )
```
